256 devices in a mesh: lev: 8 (over y, core), gx: 4 (over z_hi), gy: 8 (over z_lo, x).
Axes of the slice: x: 4, y: 4, z: 8 (z_hi: 4, z_lo: 2; z = z_hi * 2 + z_lo), core: 2. Of those that a mesh axis runs over, the one named last changes fastest.
Arguments:
- ensemble: float32 [96, 64, 16, 1024], P(None, 'lev', 'gx', 'gy'), may hold values from -6 to 6
- level_scale: float32 [64], P('lev'), may hold values from 0.3 to 1.5
- channel_weights: float32 [4, 64], P(None, 'lev'), may hold values from 0.2 to 1
- error_var: float32 [4], replicated, may hold values from 0.5 to 4
- observed: float32 [2, 4, 512], replicated, may hold values from -8 to 8
- column_x: int32 [2, 512], replicated, may hold values from 0 to 3
- column_y: int32 [2, 512], replicated, may hold values from 0 to 127
- peak_level: int32 [2, 512], replicated, may hold values from 0 to 63
- owner_map: int32 [2], replicated, may hold values from 0 to 31
- courant_x: float32 [64, 16, 1024], P('lev', 'gx', 'gy'), may hold values from -0.3 to 0.3
- courant_y: float32 [64, 16, 1024], P('lev', 'gx', 'gy'), may hold values from -0.3 to 0.3
Outputs:
- analysis: float32 [96, 64, 16, 1024], P(None, 'lev', 'gx', 'gy')
The draws below stay inside these ranges and needn't reach their ends.
Inputs may be any that keep to these rules, and one draw needn't show every extreme that they name: `owner_map`: block o of columns holds first-dimension columns (o // 8) * 4 onward and second-dimension columns (o % 8) * 128 onward.
All inputs are finite; a program needn't handle non-finite values.
Results may differ from the reference program's by a relative error of at most 0.008.
The reference program's roundings to bfloat16 on the way (of `anomaly` and `weight`) count: a program that leaves them out, or rounds other values in their place, can miss the bound.
Values may be sent and summed in bfloat16 or wider, within the bound.
A program may use at most 64 MiB of HBM per device.

```python
import math
import jax
import jax.numpy as jnp
from jax import lax

M = 96
CX = 4
CY = 128
NB = 512
NCH = 4
NBLK = 2
L = 64
NX = 16
NY = 1024
HORIZ = 32
PEAKW = 32
VLOC = 16
HLOC_X = 8
HLOC_Y = 512


def set_ends(array, stream_key, smallest, largest):
    index_at = [jax.random.randint(jax.random.fold_in(stream_key, axis), (), 0, length) for axis, length in enumerate(array.shape)]
    longest = array.shape.index(max(array.shape))
    neighbour = index_at[:longest] + [(index_at[longest] + 1) % array.shape[longest]] + index_at[longest + 1:]
    return array.at[tuple(index_at)].set(smallest).at[tuple(neighbour)].set(largest)


def steps_of(key, shape, split, least, high):
    level, own = 1.0, jax.random.fold_in(key, 6)
    for position, shards_of in split:
        heights = jnp.exp(jax.random.uniform(jax.random.fold_in(own, position), (shards_of,), jnp.float32, least / len(split), high / len(split)))
        level = level * jnp.repeat(heights, shape[position] // shards_of).reshape([-1 if axis == position else 1 for axis in range(len(shape))])
    return level


def scatter_about(stream_key, shape, width, reach, split=(), held_as=jnp.bfloat16):
    drawn = jax.random.normal(stream_key, shape, jnp.float32) * width
    if len(split) > 0:
        drawn = steps_of(stream_key, shape, split, -0.22, 0.18) * drawn
    return jnp.clip(drawn, min=-reach, max=reach).astype(held_as)


def setup_inputs(seed: int = 0) -> dict:
    splits = jax.random.split(jax.random.key(seed), 12)
    ensemble = scatter_about(splits[0], (M, L, NX, NY), 1.0, 6.0, ((1, 8), (2, 4), (3, 8)), jnp.float32)
    level_scale = jnp.clip(jnp.exp(math.log(1.5) - 1.60943787 * jax.random.uniform(splits[1], (L,), jnp.float32) ** steps_of(splits[1], (L,), ((0, 8),), -0.2, 0.2)), 0.3, 1.5)
    channel_weights = jnp.clip(jnp.exp(math.log(1.0) - 1.609438 * jax.random.uniform(splits[2], (NCH, L), jnp.float32) ** steps_of(splits[2], (NCH, L), ((1, 8),), -0.2, 0.2)), 0.2, 1.0)
    error_var = jnp.clip(jnp.exp(jax.random.uniform(splits[3], (NCH,), jnp.float32, math.log(0.5), math.log(4.0))), 0.5, 4.0)
    observed = scatter_about(splits[4], (NBLK, NCH, NB), 2.0, 8.0, (), jnp.float32)
    column_x = set_ends(jax.random.randint(splits[5], (NBLK, NB), 0, CX), jax.random.fold_in(splits[5], 1), 0, CX - 1).astype(jnp.int32)
    column_y = set_ends(jax.random.randint(splits[6], (NBLK, NB), 0, CY), jax.random.fold_in(splits[6], 1), 0, CY - 1).astype(jnp.int32)
    peak_level = set_ends(jax.random.randint(splits[7], (NBLK, NB), 0, L), jax.random.fold_in(splits[7], 1), 0, L - 1).astype(jnp.int32)
    owner_map = jax.random.randint(splits[8], (NBLK,), 0, HORIZ).astype(jnp.int32)
    courant_x = jnp.clip(jax.random.uniform(splits[9], (L, NX, NY), jnp.float32, -0.3, 0.3) * steps_of(splits[9], (L, NX, NY), ((0, 8), (1, 4), (2, 8)), -0.4, 0.0), -0.3, 0.3)
    courant_y = jnp.clip(jax.random.uniform(splits[10], (L, NX, NY), jnp.float32, -0.3, 0.3) * steps_of(splits[10], (L, NX, NY), ((0, 8), (1, 4), (2, 8)), -0.4, 0.0), -0.3, 0.3)
    return dict(ensemble=ensemble, level_scale=level_scale, channel_weights=channel_weights, error_var=error_var, observed=observed, column_x=column_x, column_y=column_y, peak_level=peak_level, owner_map=owner_map, courant_x=courant_x, courant_y=courant_y)


KAPPA = 0.1
HIGHEST = lax.Precision.HIGHEST

def periodic_gap(first_pos, second_pos, extent):
    raw_gap = jnp.abs(first_pos - second_pos) % extent
    return jnp.minimum(raw_gap, extent - raw_gap).astype(jnp.float32)

def solve_spd(matrix, right_side):
    factor = jnp.linalg.cholesky(matrix)
    inner_part = lax.linalg.triangular_solve(factor, right_side, left_side=True, lower=True)
    return lax.linalg.triangular_solve(factor, inner_part, left_side=True, lower=True, transpose_a=True)

def stencil_terms(centre, west, east, south, north, speed_x, speed_y):
    return centre - jnp.maximum(speed_x, 0.0) * (centre - west) - jnp.minimum(speed_x, 0.0) * (east - centre) - jnp.maximum(speed_y, 0.0) * (centre - south) - jnp.minimum(speed_y, 0.0) * (north - centre) + KAPPA * (east + west + north + south - 4.0 * centre)

def advect(field, speed_x, speed_y):
    return stencil_terms(field, jnp.roll(field, 1, axis=2), jnp.roll(field, -1, axis=2), jnp.roll(field, 1, axis=3), jnp.roll(field, -1, axis=3), speed_x, speed_y)

def evolve(current, level_scale, channel_weights, column_xs, column_ys, levels):
    members = current.shape[0]
    profile = jnp.tanh(current[:, :, column_xs, column_ys] * level_scale[None, :, None])
    level_pos = jnp.arange(L, dtype=jnp.int32).astype(jnp.float32)
    peak_shape = jnp.exp(-jnp.square((level_pos[:, None] - levels[None, :].astype(jnp.float32)) / PEAKW))
    kernel = channel_weights[:, :, None] * peak_shape[None, :, :]
    evolved = jnp.einsum('mlj,klj->mkj', profile, kernel, precision=HIGHEST)
    return evolved.reshape(members, NCH * NB)

def block_weights(evolved, observed_row, error_inv):
    members = evolved.shape[0]
    mean_sim = jnp.mean(evolved, axis=0)
    spread = evolved - mean_sim
    innovation = observed_row - mean_sim
    scaled = spread * error_inv
    cross_term = jnp.dot(scaled, spread.T, precision=HIGHEST)
    pull_vec = jnp.dot(scaled, innovation, precision=HIGHEST)
    system = (members - 1) * jnp.eye(members, dtype=jnp.float32) + cross_term
    combined = solve_spd(system, (pull_vec[None, :] - 0.5 * cross_term).T).T
    increments = error_inv * (innovation - 0.5 * spread) - jnp.dot(combined, scaled, precision=HIGHEST)
    return (spread.astype(jnp.bfloat16), increments.astype(jnp.bfloat16))

def regress(current, block_pert, block_solved, obs_xs, obs_ys, obs_levels):
    members = current.shape[0]
    anomaly = (current - jnp.mean(current, axis=0, keepdims=True)).astype(jnp.bfloat16)
    grid_x = jnp.arange(NX, dtype=jnp.int32)
    grid_y = jnp.arange(NY, dtype=jnp.int32)
    taper_x = jnp.exp(-jnp.square(periodic_gap(grid_x[:, None], obs_xs[None, :], NX) / HLOC_X))
    taper_y = jnp.exp(-jnp.square(periodic_gap(grid_y[:, None], obs_ys[None, :], NY) / HLOC_Y))
    obs_level = obs_levels.astype(jnp.float32)

    def one_level(level_now):
        level_rows = lax.dynamic_index_in_dim(anomaly, level_now, 1, keepdims=False).reshape(members, NX * NY)
        taper_v = jnp.exp(-jnp.square((level_now.astype(jnp.float32) - obs_level) / VLOC))
        taper = (taper_v[None, None, :] * taper_x[:, None, :] * taper_y[None, :, :]).reshape(NX * NY, -1)
        covariance = lax.dot_general(level_rows.astype(jnp.float32), block_pert.astype(jnp.float32), (((0,), (0,)), ((), ())), preferred_element_type=jnp.float32)
        weight = (taper * covariance / (members - 1)).astype(jnp.bfloat16)
        return lax.dot_general(block_solved.astype(jnp.float32), weight.astype(jnp.float32), (((1,), (1,)), ((), ())), preferred_element_type=jnp.float32)
    increment = lax.map(one_level, jnp.arange(L, dtype=jnp.int32))
    increment = jnp.transpose(increment, (1, 0, 2)).reshape(current.shape)
    return current + increment

def reference(ensemble, level_scale, channel_weights, error_var, observed, column_x, column_y, peak_level, owner_map, courant_x, courant_y):
    current = ensemble
    blocks_y = NY // CY
    error_inv = jnp.repeat(1.0 / error_var, NB)
    for block_index in range(NBLK):
        owner_rank = owner_map[block_index]
        column_xs = owner_rank // blocks_y * CX + column_x[block_index]
        column_ys = owner_rank % blocks_y * CY + column_y[block_index]
        levels = peak_level[block_index]
        evolved = evolve(current, level_scale, channel_weights, column_xs, column_ys, levels)
        block_pert, block_solved = block_weights(evolved, observed[block_index].reshape(NCH * NB), error_inv)
        current = regress(current, block_pert, block_solved, jnp.tile(column_xs, NCH), jnp.tile(column_ys, NCH), jnp.tile(levels, NCH))
    for turn_index in range(2):
        current = advect(current, courant_x, courant_y)
    return current
```

```python
import jax
import jax.numpy as jnp
from jax import lax
from jax.experimental import pallas as pl
from jax.experimental.pallas import tpu as pltpu
from jax.sharding import PartitionSpec as P

NB = 512
NCH = 4
NBLK = 2
PEAKW = 32
VLOC = 16
HLOC_X = 8
HLOC_Y = 512
KAPPA = 0.1

M = 96
LEV = 8
CX = 4
CY = 128
COLS = CX * CY
ROWS = LEV * CX
HALF = 256
PIECE = 24

F32 = jnp.float32
BF16 = jnp.bfloat16
HIGHEST = lax.Precision.HIGHEST
MESH = pl.DeviceIdType.MESH
VMEM_LIMIT = 56 * 1024 * 1024


def split3(value):
    high = value.astype(BF16)
    rest = value - high.astype(F32)
    middle = rest.astype(BF16)
    low = (rest - middle.astype(F32)).astype(BF16)
    return high, middle, low


def partial_kernel(scale_ref, weight_ref, state_ref, column_ref, peak_ref, out_ref, gathered):
    first_level = (lax.axis_index("lev") * LEV).astype(F32)
    chosen = (lax.broadcasted_iota(jnp.int32, (COLS, NB), 0) == column_ref[...]).astype(F32)
    chosen = chosen.astype(BF16)
    for level in range(LEV):
        profile = jnp.concatenate(
            [jnp.tanh(state_ref[level * CX + x] * scale_ref[level]) for x in range(CX)], axis=1
        )
        parts = jnp.concatenate(split3(profile), axis=0)
        picked = jnp.dot(parts, chosen, preferred_element_type=F32)
        gathered[level] = picked[:M] + picked[M : 2 * M] + picked[2 * M :]
    peak = peak_ref[...].astype(F32)
    shapes = [
        jnp.exp(-jnp.square((first_level + level - peak) / PEAKW)) for level in range(LEV)
    ]
    for tile in range(4):
        lanes = slice(tile * 128, tile * 128 + 128)
        for channel in range(NCH):
            total = jnp.zeros((M, 128), F32)
            for level in range(LEV):
                total += gathered[level, :, lanes] * (
                    shapes[level][:, lanes] * weight_ref[channel, level]
                )
            half, quarter = tile // 2, tile % 2
            out_ref[half, channel, quarter * M : quarter * M + M, :] = total


def device_at(x, z, lev):
    return (lev, lax.div(z, 2), lax.rem(z, 2) * 4 + x)


def share_kernel(
    owner_ref, part_ref, out_ref, from_core, sums, from_y, from_z, from_x, send, recv
):
    lev = lax.axis_index("lev")
    gx = lax.axis_index("gx")
    gy = lax.axis_index("gy")
    core, y = lax.rem(lev, 2), lax.div(lev, 2)
    x, z = lax.rem(gy, 4), gx * 2 + lax.div(gy, 4)
    other = y * 2 + 1 - core
    owner = owner_ref[0]
    owner_z = lax.div(owner, 8) * 2 + lax.div(lax.rem(owner, 8), 4)
    owner_x = lax.rem(owner, 4)

    y_at = lambda d: lax.rem(y + d, 4)
    z_at = lambda d: lax.rem(z + d, 8)
    x_at = lambda d: lax.rem(x + d, 4)
    to_core = device_at(x, z, other)
    to_y = lambda d: device_at(x, z, y_at(d) * 2 + core)
    to_z = lambda d: device_at(x, z_at(d), lev)
    to_x = lambda d: device_at(x_at(d), z, lev)

    barrier = pltpu.get_barrier_semaphore()
    peers = [to_core] + [to_y(d) for d in range(1, 4)]
    peers += [to_z(d) for d in range(1, 8)] + [to_x(d) for d in range(1, 4)]
    for peer in peers:
        pl.semaphore_signal(barrier, inc=1, device_id=peer, device_id_type=MESH)
    pl.semaphore_wait(barrier, len(peers))

    slot = [0]

    def start(src, dst, device):
        number = slot[0]
        slot[0] += 1
        copy = pltpu.make_async_remote_copy(
            src_ref=src,
            dst_ref=dst,
            send_sem=send.at[number],
            recv_sem=recv.at[number],
            device_id=device,
            device_id_type=MESH,
        )
        copy.start()
        return copy

    started = []
    order = (1, 2, 3, 0)
    core_copies = [
        start(part_ref.at[1 - core, y_at(d)], from_core.at[y_at(d)], to_core) for d in order
    ]
    y_copies = []
    for d, copy in zip(order, core_copies):
        copy.wait_recv()
        where = y_at(d)
        sums[where] = part_ref[core, where] + from_core[where]
        if d > 0:
            y_copies.append(start(sums.at[where], from_y.at[d - 1], to_y(d)))
    started += core_copies + y_copies
    for copy in y_copies:
        copy.wait_recv()
    total = sums[y] + from_y[0] + from_y[1] + from_y[2]
    sums[y] = total

    z_copies = [
        start(sums.at[y, pl.ds(z_at(d) * PIECE, PIECE)], from_z.at[z], to_z(d))
        for d in range(1, 8)
    ]
    from_z[z] = sums[y, pl.ds(pl.multiple_of(z * PIECE, 8), PIECE)]
    for copy in z_copies:
        copy.wait_recv()
    started += z_copies
    from_x[x] = from_z[owner_z]
    x_copies = [start(from_x.at[x], from_x.at[x], to_x(d)) for d in range(1, 4)]
    for copy in x_copies:
        copy.wait_recv()
    started += x_copies

    mine = pl.ds(pl.multiple_of(z * PIECE, 8), PIECE)
    out_ref[core, y, mine] = from_x[owner_x]
    z_copies = [
        start(out_ref.at[core, y, mine], out_ref.at[core, y, mine], to_z(d)) for d in range(1, 8)
    ]
    for copy in z_copies:
        copy.wait_recv()
    started += z_copies
    y_copies = [
        start(out_ref.at[core, y], out_ref.at[core, y], to_y(d)) for d in range(1, 4)
    ]
    core_copies = [start(out_ref.at[core, y], out_ref.at[core, y], to_core)]
    for d, copy in zip(range(1, 4), y_copies):
        copy.wait_recv()
        came = out_ref.at[core, y_at(4 - d)]
        core_copies.append(start(came, came, to_core))
    for copy in core_copies:
        copy.wait_recv()
    started += y_copies + core_copies
    for copy in started:
        copy.wait_send()


N_COPIES = 4 + 3 + 7 + 3 + 7 + 3 + 4


def update_kernel(
    owner_ref,
    inverse_ref,
    state_ref,
    evolved_ref,
    observed_ref,
    column_x_ref,
    column_y_ref,
    peak_ref,
    out_ref,
    spread,
    scaled,
    innovation,
    pert,
    solved_t,
    taper_y,
    taper_vx,
    weight,
):
    owner = owner_ref[0]
    for channel in range(NCH):
        inverse = inverse_ref[channel]
        for tile in range(4):
            half, quarter = tile // 2, tile % 2
            evolved = evolved_ref[half, channel, quarter * M : quarter * M + M, :]
            mean = jnp.sum(evolved, axis=0, keepdims=True) * (1.0 / M)
            lanes = slice(channel * NB + tile * 128, channel * NB + tile * 128 + 128)
            part = evolved - mean
            spread[:, lanes] = part
            pert[:, lanes] = part.astype(BF16)
            scaled[:M, lanes] = part * inverse
            away = observed_ref[channel : channel + 1, tile * 128 : tile * 128 + 128] - mean
            innovation[:, lanes] = away
            scaled[M:, lanes] = jnp.broadcast_to(away * inverse, (8, 128))
    cross = lax.dot_general(
        scaled[...], spread[...], (((1,), (1,)), ((), ())), precision=HIGHEST,
        preferred_element_type=F32,
    )
    lane = lax.broadcasted_iota(jnp.int32, (M + 8, 128), 1)
    row = lax.broadcasted_iota(jnp.int32, (M + 8, 128), 0)
    cross = jnp.concatenate([cross, jnp.zeros((M + 8, 128 - M), F32)], axis=1)
    system = cross + jnp.where((lane == row) & (row < M), float(M - 1), 0.0)

    def sweep(pivot, matrix):
        at_row, at_lane = row == pivot, lane == pivot
        pivot_row = jnp.sum(jnp.where(at_row, matrix, 0.0), axis=0, keepdims=True)
        column = jnp.sum(jnp.where(at_lane, matrix, 0.0), axis=1, keepdims=True)
        first = lane[:1] == pivot
        corner = jnp.sum(jnp.where(first, pivot_row, 0.0), axis=1, keepdims=True)
        scale = 1.0 / corner
        times = jnp.where(first, -1.0, pivot_row) * scale
        column = jnp.where(row[:, :1] == pivot, -1.0, column)
        return jnp.where(at_row | at_lane, 0.0, matrix) - column * times

    swept = lax.fori_loop(0, M, sweep, system)
    gain = (swept[M : M + 1] - 0.5 * (M - 1) * swept[:M])[:, :M]
    for channel in range(NCH):
        lanes = slice(channel * NB, channel * NB + NB)
        change = jnp.dot(gain, spread[:, lanes], precision=HIGHEST, preferred_element_type=F32)
        solved = inverse_ref[channel] * (innovation[:, lanes] - change)
        solved_t[lanes, :] = solved.T.astype(BF16)

    peak = peak_ref[...].astype(F32)
    at_x = lax.div(owner, 8) * CX + column_x_ref[...]
    at_y = lax.rem(owner, 8) * CY + column_y_ref[...]
    grid_y = lax.axis_index("gy") * CY + lax.broadcasted_iota(jnp.int32, (CY, NB), 0)
    gap = jnp.abs(grid_y - at_y)
    gap = jnp.minimum(gap, 8 * CY - gap).astype(F32)
    taper_y[...] = jnp.exp(-jnp.square(gap / HLOC_Y))
    index = lax.broadcasted_iota(jnp.int32, (ROWS, NB), 0)
    grid_x = lax.axis_index("gx") * CX + lax.rem(index, CX)
    gap = jnp.abs(grid_x - at_x)
    gap = jnp.minimum(gap, 4 * CX - gap).astype(F32)
    level = (lax.axis_index("lev") * LEV + lax.div(index, CX)).astype(F32)
    taper_vx[...] = (
        jnp.exp(-jnp.square((level - peak) / VLOC)) * jnp.exp(-jnp.square(gap / HLOC_X))
    ) * (1.0 / (M - 1))

    @pl.loop(0, ROWS)
    def _(at):
        state = state_ref[at]
        anomaly = (state - jnp.sum(state, axis=0, keepdims=True) * (1.0 / M)).T.astype(BF16)
        beside = taper_vx[pl.ds(at, 1), :]
        for chunk in range(NB // HALF):
            near = slice(chunk * HALF, chunk * HALF + HALF)
            taper = taper_y[:, near] * beside[:, near]
            for channel in range(NCH):
                lanes = slice(channel * NB + chunk * HALF, channel * NB + chunk * HALF + HALF)
                covariance = jnp.dot(anomaly, pert[:, lanes], preferred_element_type=F32)
                weight[:, lanes] = (taper * covariance).astype(BF16)
        update = jnp.dot(weight[...], solved_t[...], preferred_element_type=F32)
        out_ref[at] = state + update.T


def stencil_kernel(
    speed_x_ref, speed_y_ref, state_ref, out_ref, middle, face, got, edge, came, send, recv
):
    lev = lax.axis_index("lev")
    gx = lax.axis_index("gx")
    gy = lax.axis_index("gy")
    up_x = (lev, lax.rem(gx + 1, 4), gy)
    down_x = (lev, lax.rem(gx + 3, 4), gy)
    up_y = (lev, gx, lax.rem(gy + 1, 8))
    down_y = (lev, gx, lax.rem(gy + 7, 8))
    targets = (up_x, down_x, up_y, down_y)
    barrier = pltpu.get_barrier_semaphore()
    for peer in targets:
        pl.semaphore_signal(barrier, inc=1, device_id=peer, device_id_type=MESH)
    pl.semaphore_wait(barrier, 4)
    lane = lax.broadcasted_iota(jnp.int32, (M, CY), 1)

    for turn in range(2):
        source = state_ref if turn == 0 else middle
        target = middle if turn == 0 else out_ref

        def start(number, src, dst):
            copy = pltpu.make_async_remote_copy(
                src_ref=src,
                dst_ref=dst,
                send_sem=send.at[turn, number],
                recv_sem=recv.at[turn, number],
                device_id=targets[number],
                device_id_type=MESH,
            )
            copy.start()
            return copy

        def pack(level, carry):
            last, first = carry
            face[turn, 0, level] = source[level * CX + CX - 1].astype(BF16)
            face[turn, 1, level] = source[level * CX].astype(BF16)
            for x in range(CX):
                tile = source[level * CX + x]
                here = lane == level * CX + x
                last = jnp.where(here, tile[:, CY - 1 :], last)
                first = jnp.where(here, tile[:, :1], first)
            return last, first

        nothing = jnp.zeros((M, CY), F32)
        last, first = lax.fori_loop(0, LEV, pack, (nothing, nothing))
        edge[turn, 0] = last
        edge[turn, 1] = first
        copies = [start(n, face.at[turn, n], got.at[turn, n]) for n in range(2)]
        copies += [start(2 + n, edge.at[turn, n], came.at[turn, n]) for n in range(2)]
        for copy in copies:
            copy.wait()

        @pl.loop(0, LEV)
        def _(level):
            shift = lax.rem(CY - level * CX, CY)
            souths = pltpu.roll(came[turn, 0], shift, 1)
            norths = pltpu.roll(came[turn, 1], shift, 1)
            for x in range(CX):
                at = level * CX + x
                centre = source[at]
                west = source[at - 1] if x > 0 else got[turn, 0, level].astype(F32)
                east = source[at + 1] if x < CX - 1 else got[turn, 1, level].astype(F32)
                south = jnp.where(lane == 0, souths[:, x : x + 1], pltpu.roll(centre, 1, 1))
                north = jnp.where(
                    lane == CY - 1, norths[:, x : x + 1], pltpu.roll(centre, CY - 1, 1)
                )
                u = speed_x_ref[pl.ds(at, 1), :]
                v = speed_y_ref[pl.ds(at, 1), :]
                target[at] = (
                    centre * (1.0 - 4.0 * KAPPA - jnp.abs(u) - jnp.abs(v))
                    + west * (jnp.maximum(u, 0.0) + KAPPA)
                    + east * (KAPPA - jnp.minimum(u, 0.0))
                    + south * (jnp.maximum(v, 0.0) + KAPPA)
                    + north * (KAPPA - jnp.minimum(v, 0.0))
                )


SMEM_SPEC = pl.BlockSpec(memory_space=pltpu.SMEM)
VMEM_SPEC = pl.BlockSpec(memory_space=pltpu.VMEM)


def partial(scale, weights, state, column, peak):
    return pl.pallas_call(
        partial_kernel,
        out_shape=jax.ShapeDtypeStruct((2, NCH, 2 * M, 128), F32),
        in_specs=[SMEM_SPEC] * 2 + [VMEM_SPEC] * 3,
        out_specs=VMEM_SPEC,
        scratch_shapes=[pltpu.VMEM((LEV, M, NB), F32)],
        compiler_params=pltpu.CompilerParams(vmem_limit_bytes=VMEM_LIMIT),
        name="partial",
    )(scale, weights, state, column, peak)


def share(number, owner, part):
    return pl.pallas_call(
        share_kernel,
        out_shape=jax.ShapeDtypeStruct((2, NCH, 2 * M, 128), F32),
        in_specs=[SMEM_SPEC, VMEM_SPEC],
        out_specs=VMEM_SPEC,
        scratch_shapes=[
            pltpu.VMEM((4, 2 * M, 128), F32),
            pltpu.VMEM((4, 2 * M, 128), F32),
            pltpu.VMEM((3, 2 * M, 128), F32),
            pltpu.VMEM((8, PIECE, 128), F32),
            pltpu.VMEM((4, PIECE, 128), F32),
            pltpu.SemaphoreType.DMA((N_COPIES,)),
            pltpu.SemaphoreType.DMA((N_COPIES,)),
        ],
        compiler_params=pltpu.CompilerParams(
            vmem_limit_bytes=VMEM_LIMIT, collective_id=number, has_side_effects=True
        ),
        name="share",
    )(owner, part)


def update(owner, inverse, state, evolved, observed, column_x, column_y, peak):
    return pl.pallas_call(
        update_kernel,
        out_shape=jax.ShapeDtypeStruct((ROWS, M, CY), F32),
        in_specs=[SMEM_SPEC] * 2 + [VMEM_SPEC] * 6,
        out_specs=VMEM_SPEC,
        scratch_shapes=[
            pltpu.VMEM((M, NCH * NB), F32),
            pltpu.VMEM((M + 8, NCH * NB), F32),
            pltpu.VMEM((1, NCH * NB), F32),
            pltpu.VMEM((M, NCH * NB), BF16),
            pltpu.VMEM((NCH * NB, M), BF16),
            pltpu.VMEM((CY, NB), F32),
            pltpu.VMEM((ROWS, NB), F32),
            pltpu.VMEM((CY, NCH * NB), BF16),
        ],
        compiler_params=pltpu.CompilerParams(vmem_limit_bytes=VMEM_LIMIT),
        name="update",
    )(owner, inverse, state, evolved, observed, column_x, column_y, peak)


def transport(speed_x, speed_y, state):
    return pl.pallas_call(
        stencil_kernel,
        out_shape=jax.ShapeDtypeStruct((ROWS, M, CY), F32),
        in_specs=[VMEM_SPEC] * 3,
        out_specs=VMEM_SPEC,
        scratch_shapes=[
            pltpu.VMEM((ROWS, M, CY), F32),
            pltpu.VMEM((2, 2, LEV, M, CY), BF16),
            pltpu.VMEM((2, 2, LEV, M, CY), BF16),
            pltpu.VMEM((2, 2, M, CY), F32),
            pltpu.VMEM((2, 2, M, CY), F32),
            pltpu.SemaphoreType.DMA((2, 4)),
            pltpu.SemaphoreType.DMA((2, 4)),
        ],
        compiler_params=pltpu.CompilerParams(
            vmem_limit_bytes=VMEM_LIMIT, collective_id=NBLK, has_side_effects=True
        ),
        name="transport",
    )(speed_x, speed_y, state)


def shards(
    ensemble,
    level_scale,
    channel_weights,
    error_var,
    observed,
    column_x,
    column_y,
    peak_level,
    owner_map,
    courant_x,
    courant_y,
):
    state = ensemble.reshape(M, ROWS, CY).transpose(1, 0, 2)
    inverse = 1.0 / error_var
    columns = column_x * CY + column_y
    for block in range(NBLK):
        one = slice(block, block + 1)
        owner, peak = owner_map[one], peak_level[one]
        part = partial(level_scale, channel_weights, state, columns[one], peak)
        evolved = share(block, owner, part)
        state = update(
            owner, inverse, state, evolved, observed[block], column_x[one], column_y[one], peak
        )
    result = transport(courant_x.reshape(ROWS, CY), courant_y.reshape(ROWS, CY), state)
    return result.transpose(1, 0, 2).reshape(ensemble.shape)


def solution(mesh):
    in_specs = (
        P(None, "lev", "gx", "gy"),
        P("lev"),
        P(None, "lev"),
        P(),
        P(),
        P(),
        P(),
        P(),
        P(),
        P("lev", "gx", "gy"),
        P("lev", "gx", "gy"),
    )
    out_specs = P(None, "lev", "gx", "gy")
    return jax.shard_map(shards, mesh=mesh, in_specs=in_specs, out_specs=out_specs, check_vma=False)
```

```python
import jax
import jax.numpy as jnp
from jax import lax
from jax.experimental import pallas as pl
from jax.experimental.pallas import tpu as pltpu
from jax.sharding import PartitionSpec as P

NB = 512
NCH = 4
NBLK = 2
PEAKW = 32
VLOC = 16
HLOC_X = 8
HLOC_Y = 512
KAPPA = 0.1

M = 96
LEV = 8
CX = 4
CY = 128
COLS = CX * CY
ROWS = LEV * CX
HALF = 256
GROUP = 4
LAST = 8
STEPS = M // ROWS * GROUP
PIECE = 24
SOME = LAST // CX
N_FACES = 2 * (2 * (LEV // SOME) + 2)

F32 = jnp.float32
BF16 = jnp.bfloat16
HIGHEST = lax.Precision.HIGHEST
MESH = pl.DeviceIdType.MESH
VMEM_LIMIT = 56 * 1024 * 1024


def split3(value):
    high = value.astype(BF16)
    rest = value - high.astype(F32)
    middle = rest.astype(BF16)
    low = (rest - middle.astype(F32)).astype(BF16)
    return high, middle, low


def radiances(block, scale_ref, weight_ref, state, column_x_ref, column_y_ref, peak_ref, part, gathered):
    one = slice(block, block + 1)
    column = column_x_ref[one, :] * CY + column_y_ref[one, :]
    first_level = (lax.axis_index("lev") * LEV).astype(F32)
    chosen = (lax.broadcasted_iota(jnp.int32, (COLS, NB), 0) == column).astype(F32)
    chosen = chosen.astype(BF16)
    for level in range(LEV):
        profile = jnp.concatenate(
            [jnp.tanh(state[level * CX + x] * scale_ref[level]) for x in range(CX)], axis=1
        )
        parts = jnp.concatenate(split3(profile), axis=0)
        picked = jnp.dot(parts, chosen, preferred_element_type=F32)
        gathered[level] = picked[:M] + picked[M : 2 * M] + picked[2 * M :]
    peak = peak_ref[one, :].astype(F32)
    shapes = [
        jnp.exp(-jnp.square((first_level + level - peak) / PEAKW)) for level in range(LEV)
    ]

    def produce(channel):
        factors = [shapes[level] * weight_ref[channel, level] for level in range(LEV)]
        for tile in range(4):
            lanes = slice(tile * 128, tile * 128 + 128)
            half, quarter = tile // 2, tile % 2
            total = gathered[0, :, lanes] * factors[0][:, lanes]
            for level in range(1, LEV):
                total += gathered[level, :, lanes] * factors[level][:, lanes]
            part[half, channel, quarter * M : quarter * M + M, :] = total

    return produce


def place():
    lev, gx, gy = lax.axis_index("lev"), lax.axis_index("gx"), lax.axis_index("gy")
    core, y = lax.rem(lev, 2), lax.div(lev, 2)
    x, z = lax.rem(gy, 4), gx * 2 + lax.div(gy, 4)

    def at(dx, dy, dz, dcore):
        there_x, there_y = lax.rem(x + dx, 4), lax.rem(y + dy, 4)
        there_z, there_core = lax.rem(z + dz, 8), lax.rem(core + dcore, 2)
        return (
            there_y * 2 + there_core,
            lax.div(there_z, 2),
            lax.rem(there_z, 2) * 4 + there_x,
        )

    beside = (
        (lev, lax.rem(gx + 1, 4), gy),
        (lev, lax.rem(gx + 3, 4), gy),
        (lev, gx, lax.rem(gy + 1, 8)),
        (lev, gx, lax.rem(gy + 7, 8)),
    )
    return x, y, z, core, at, beside


def share(block, produce, owner_ref, part, whole, from_core, sums, from_y, from_z, from_x, send, recv):
    x, y, z, core, at, _ = place()
    owner = owner_ref[block]
    owner_z = lax.div(owner, 8) * 2 + lax.div(lax.rem(owner, 8), 4)
    owner_x = lax.rem(owner, 4)
    y_at = lambda d: lax.rem(y + d, 4)
    z_at = lambda d: lax.rem(z + d, 8)
    to_core = at(0, 0, 0, 1)
    to_x = lambda d: at(d, 0, 0, 0)
    to_y = lambda d: at(0, d, 0, 0)
    to_z = lambda d: at(0, 0, d, 0)
    slot = [0]
    started = []

    def start(src, dst, device):
        number = slot[0]
        slot[0] += 1
        copy = pltpu.make_async_remote_copy(
            src_ref=src,
            dst_ref=dst,
            send_sem=send.at[block, number],
            recv_sem=recv.at[block, number],
            device_id=device,
            device_id_type=MESH,
        )
        copy.start()
        started.append(copy)
        return copy

    def arrive(copies):
        for copy in copies:
            copy.wait_recv()

    sent = []

    def pass_on(d, copy):
        copy.wait_recv()
        here = y_at(d)
        sums[here] = part[core, here] + from_core[here]
        if d > 0:
            sent.append(start(sums.at[here], from_y.at[d - 1], to_y(d)))

    before = None
    for d in (2, 1, 3, 0):
        produce(y_at(d))
        copy = start(part.at[1 - core, y_at(d)], from_core.at[y_at(d)], to_core)
        if before is not None:
            pass_on(*before)
        before = d, copy
    pass_on(*before)
    arrive(sent)
    sums[y] = sums[y] + from_y[0] + from_y[1] + from_y[2]

    far_first = (4, 3, 5, 2, 6, 1, 7)
    sent = [
        start(sums.at[y, pl.ds(z_at(d) * PIECE, PIECE)], from_z.at[z], to_z(d))
        for d in far_first
    ]
    mine = pl.ds(pl.multiple_of(z * PIECE, 8), PIECE)
    from_z[z] = sums[y, mine]
    arrive(sent)
    from_x[x] = from_z[owner_z]
    own = from_x.at[x]
    arrive([start(own, own, to_x(d)) for d in (2, 1, 3)])
    whole[core, y, mine] = from_x[owner_x]
    own = whole.at[core, y, mine]
    arrive([start(own, own, to_z(d)) for d in far_first])
    own = whole.at[core, y]
    sent = [start(own, own, to_y(d)) for d in (2, 1, 3)]
    flying = [start(own, own, to_core)]
    for d, copy in zip((2, 1, 3), sent):
        copy.wait_recv()
        came = whole.at[core, y_at(4 - d)]
        flying.append(start(came, came, to_core))
    arrive(flying)
    for copy in started:
        copy.wait_send()


N_COPIES = 4 + 3 + 7 + 3 + 7 + 3 + 4


def assimilate(
    block,
    owner_ref,
    error_ref,
    state,
    whole,
    observed_ref,
    column_x_ref,
    column_y_ref,
    peak_ref,
    spread,
    scaled,
    innovation,
    pert,
    solved_t,
    taper_y,
    taper_vx,
    system,
    weight,
    then,
):
    owner = owner_ref[block]
    one = slice(block, block + 1)
    inverses = [1.0 / jnp.full((1, 128), error_ref[channel], F32) for channel in range(NCH)]
    for channel in range(NCH):
        inverse = inverses[channel]
        for tile in range(4):
            half, quarter = tile // 2, tile % 2
            evolved = whole[half, channel, quarter * M : quarter * M + M, :]
            mean = jnp.sum(evolved, axis=0, keepdims=True) * (1.0 / M)
            lanes = slice(channel * NB + tile * 128, channel * NB + tile * 128 + 128)
            part = evolved - mean
            spread[:, lanes] = part
            pert[:, lanes] = part.astype(BF16)
            scaled[:M, lanes] = part * inverse
            away = observed_ref[block, channel : channel + 1, tile * 128 : tile * 128 + 128] - mean
            innovation[:, lanes] = away
            scaled[M:, lanes] = jnp.broadcast_to(away * inverse, (8, 128))
    cross = lax.dot_general(
        scaled[...], spread[...], (((1,), (1,)), ((), ())), precision=HIGHEST,
        preferred_element_type=F32,
    )
    lane = lax.broadcasted_iota(jnp.int32, (M + 8, 128), 1)
    row = lax.broadcasted_iota(jnp.int32, (M + 8, 128), 0)
    cross = jnp.concatenate([cross, jnp.zeros((M + 8, 128 - M), F32)], axis=1)
    system[...] = cross + jnp.where((lane == row) & (row < M), float(M - 1), 0.0)

    peak = peak_ref[one, :].astype(F32)
    at_x = lax.div(owner, 8) * CX + column_x_ref[one, :]
    at_y = lax.rem(owner, 8) * CY + column_y_ref[one, :]
    grid_y = lax.axis_index("gy") * CY + lax.broadcasted_iota(jnp.int32, (CY, NB), 0)
    gap = jnp.abs(grid_y - at_y)
    gap = jnp.minimum(gap, 8 * CY - gap).astype(F32)
    taper_y[...] = jnp.exp(-jnp.square(gap / HLOC_Y))
    index = lax.broadcasted_iota(jnp.int32, (ROWS, NB), 0)
    grid_x = lax.axis_index("gx") * CX + lax.rem(index, CX)
    gap = jnp.abs(grid_x - at_x)
    gap = jnp.minimum(gap, 4 * CX - gap).astype(F32)
    level = (lax.axis_index("lev") * LEV + lax.div(index, CX)).astype(F32)
    taper_vx[...] = (
        jnp.exp(-jnp.square((level - peak) / VLOC)) * jnp.exp(-jnp.square(gap / HLOC_X))
    ) * (1.0 / (M - 1))

    def sweep(pivot):
        matrix = system[...]
        pivot_row = system[pl.ds(pivot, 1), :]
        index = jnp.full((M + 8, 128), pivot, jnp.int32)
        column = jnp.take_along_axis(matrix, index, axis=1)
        corner = jnp.take_along_axis(jnp.broadcast_to(pivot_row, (8, 128)), index[:8], axis=1)[:1]
        at_row, at_lane = row == pivot, lane == pivot
        times = jnp.where(at_lane[:1], -1.0, pivot_row) * (1.0 / corner)
        column = jnp.where(at_row, -1.0, column)
        system[...] = jnp.where(at_row | at_lane, 0.0, matrix) - column * times

    @pl.loop(0, ROWS // GROUP)
    def _(group):
        for turn in range(STEPS):
            sweep(group * STEPS + turn)
        anomalies = []
        besides = []
        for at in range(GROUP):
            member = state[group * GROUP + at]
            anomaly = member - jnp.sum(member, axis=0, keepdims=True) * (1.0 / M)
            anomalies.append(anomaly.T.astype(BF16))
            besides.append(taper_vx[pl.ds(group * GROUP + at, 1), :])
        anomaly = jnp.concatenate(anomalies, axis=0)
        for chunk in range(NB // HALF):
            near = slice(chunk * HALF, chunk * HALF + HALF)
            taper = jnp.concatenate([taper_y[:, near] * b[:, near] for b in besides], axis=0)
            for channel in range(NCH):
                lanes = slice(channel * NB + chunk * HALF, channel * NB + chunk * HALF + HALF)
                covariance = jnp.dot(anomaly, pert[:, lanes], preferred_element_type=F32)
                rows = pl.ds(group * (GROUP * CY), GROUP * CY)
                weight[rows, lanes] = (taper * covariance).astype(BF16)

    swept = system[...]
    gain = (swept[M : M + 1] - 0.5 * (M - 1) * swept[:M])[:, :M]
    for channel in range(NCH):
        lanes = slice(channel * NB, channel * NB + NB)
        change = jnp.dot(gain, spread[:, lanes], precision=HIGHEST, preferred_element_type=F32)
        solved = inverses[channel][:, :1] * (innovation[:, lanes] - change)
        solved_t[lanes, :] = solved.T.astype(BF16)

    def finish(group):
        update = jnp.dot(
            weight[pl.ds(group * (LAST * CY), LAST * CY), :],
            solved_t[...],
            preferred_element_type=F32,
        )
        for at in range(LAST):
            here = group * LAST + at
            state[here] = state[here] + update[at * CY : at * CY + CY].T

    if then is None:
        pl.loop(0, ROWS // LAST)(finish)
    else:
        for group in range(ROWS // LAST):
            finish(group)
            then(group)


def transport(speed_x_ref, speed_y_ref, state, out_ref, middle, face, got, edge, came, send, recv):
    targets = place()[-1]
    lane = lax.broadcasted_iota(jnp.int32, (M, CY), 1)
    copies = {}

    def start(key, src, dst, target):
        number = len(copies)
        copies[key] = pltpu.make_async_remote_copy(
            src_ref=src,
            dst_ref=dst,
            send_sem=send.at[number],
            recv_sem=recv.at[number],
            device_id=target,
            device_id_type=MESH,
        )
        copies[key].start()

    def send_faces(turn, group):
        source = middle if turn else state
        for level in range(group * SOME, group * SOME + SOME):
            face[turn, 0, level] = source[level * CX + CX - 1].astype(BF16)
            face[turn, 1, level] = source[level * CX].astype(BF16)
        some = pl.ds(group * SOME, SOME)
        for n in range(2):
            start(
                ("x", turn, group, n), face.at[turn, n, some], got.at[turn, n, some], targets[n]
            )

    def send_edges(turn):
        source = middle if turn else state

        def pack(level, carry):
            last, first = carry
            for x in range(CX):
                tile = source[level * CX + x]
                here = lane == level * CX + x
                last = jnp.where(here, tile[:, CY - 1 :], last)
                first = jnp.where(here, tile[:, :1], first)
            return last, first

        nothing = jnp.zeros((M, CY), F32)
        edge[turn, 0], edge[turn, 1] = lax.fori_loop(0, LEV, pack, (nothing, nothing))
        for n in range(2):
            start(("y", turn, n), edge.at[turn, n], came.at[turn, n], targets[2 + n])

    def advance(turn, level):
        source = middle if turn else state
        shift = lax.rem(CY - level * CX, CY)
        souths = pltpu.roll(came[turn, 0], shift, 1)
        norths = pltpu.roll(came[turn, 1], shift, 1)
        for x in range(CX):
            at = level * CX + x
            centre = source[at]
            west = source[at - 1] if x > 0 else got[turn, 0, level].astype(F32)
            east = source[at + 1] if x < CX - 1 else got[turn, 1, level].astype(F32)
            south = jnp.where(lane == 0, souths[:, x : x + 1], pltpu.roll(centre, 1, 1))
            north = jnp.where(lane == CY - 1, norths[:, x : x + 1], pltpu.roll(centre, CY - 1, 1))
            u = speed_x_ref[pl.ds(at, 1), :]
            v = speed_y_ref[pl.ds(at, 1), :]
            value = (
                centre * (1.0 - 4.0 * KAPPA - jnp.abs(u) - jnp.abs(v))
                + west * (jnp.maximum(u, 0.0) + KAPPA)
                + east * (KAPPA - jnp.minimum(u, 0.0))
                + south * (jnp.maximum(v, 0.0) + KAPPA)
                + north * (KAPPA - jnp.minimum(v, 0.0))
            )
            if turn == 0:
                middle[at] = value
            else:
                out_ref[pl.ds(at, M, stride=ROWS), :] = value

    def rest():
        for turn in range(2):
            send_edges(turn)
            for n in range(2):
                copies["y", turn, n].wait_recv()
            for group in range(LEV // SOME):
                for n in range(2):
                    copies["x", turn, group, n].wait_recv()
                pl.loop(group * SOME, group * SOME + SOME)(lambda level: advance(turn, level))
                if turn == 0:
                    send_faces(1, group)
        for copy in copies.values():
            copy.wait_send()

    return send_faces, rest


def filter_kernel(
    scale_ref,
    weight_ref,
    error_ref,
    owner_ref,
    ensemble_ref,
    observed_ref,
    column_x_ref,
    column_y_ref,
    peak_ref,
    speed_x_ref,
    speed_y_ref,
    out_ref,
    state,
    gathered,
    part,
    whole_0,
    whole_1,
    from_core_0,
    from_core_1,
    sums,
    from_y_0,
    from_y_1,
    from_z_0,
    from_z_1,
    from_x_0,
    from_x_1,
    spread,
    scaled,
    innovation,
    pert,
    solved_t,
    taper_y,
    taper_vx,
    system,
    weight,
    middle,
    face,
    got,
    edge,
    came,
    send,
    recv,
    face_send,
    face_recv,
):
    at, beside = place()[-2:]
    peers = [at(0, 0, 0, 1)] + [at(0, d, 0, 0) for d in range(1, 4)]
    peers += [at(0, 0, d, 0) for d in range(1, 8)] + [at(d, 0, 0, 0) for d in range(1, 4)]
    peers += beside
    barrier = pltpu.get_barrier_semaphore()
    for peer in peers:
        pl.semaphore_signal(barrier, inc=1, device_id=peer, device_id_type=MESH)

    for row in range(ROWS):
        state[row] = ensemble_ref[pl.ds(row, M, stride=ROWS), :]
    send_faces, rest = transport(
        speed_x_ref, speed_y_ref, state, out_ref, middle, face, got, edge, came, face_send,
        face_recv,
    )
    for block in range(NBLK):
        produce = radiances(
            block, scale_ref, weight_ref, state, column_x_ref, column_y_ref, peak_ref, part,
            gathered,
        )
        if block == 0:
            pl.semaphore_wait(barrier, len(peers))
        whole = (whole_0, whole_1)[block]
        from_core = (from_core_0, from_core_1)[block]
        from_y = (from_y_0, from_y_1)[block]
        from_z = (from_z_0, from_z_1)[block]
        from_x = (from_x_0, from_x_1)[block]
        share(
            block, produce, owner_ref, part, whole, from_core, sums, from_y, from_z, from_x, send,
            recv,
        )
        then = None if block < NBLK - 1 else lambda group: send_faces(0, group)
        assimilate(
            block, owner_ref, error_ref, state, whole, observed_ref, column_x_ref, column_y_ref,
            peak_ref, spread, scaled, innovation, pert, solved_t, taper_y, taper_vx, system, weight,
            then,
        )
    rest()


SMEM_SPEC = pl.BlockSpec(memory_space=pltpu.SMEM)
VMEM_SPEC = pl.BlockSpec(memory_space=pltpu.VMEM)


def shards(
    ensemble,
    level_scale,
    channel_weights,
    error_var,
    observed,
    column_x,
    column_y,
    peak_level,
    owner_map,
    courant_x,
    courant_y,
):
    result = pl.pallas_call(
        filter_kernel,
        out_shape=jax.ShapeDtypeStruct((M * ROWS, CY), F32),
        in_specs=[SMEM_SPEC] * 4 + [VMEM_SPEC] * 7,
        out_specs=VMEM_SPEC,
        scratch_shapes=[
            pltpu.VMEM((ROWS, M, CY), F32),
            pltpu.VMEM((LEV, M, NB), F32),
            pltpu.VMEM((2, NCH, 2 * M, 128), F32),
            *[pltpu.VMEM((2, NCH, 2 * M, 128), F32)] * NBLK,
            *[pltpu.VMEM((4, 2 * M, 128), F32)] * NBLK,
            pltpu.VMEM((4, 2 * M, 128), F32),
            *[pltpu.VMEM((3, 2 * M, 128), F32)] * NBLK,
            *[pltpu.VMEM((8, PIECE, 128), F32)] * NBLK,
            *[pltpu.VMEM((4, PIECE, 128), F32)] * NBLK,
            pltpu.VMEM((M, NCH * NB), F32),
            pltpu.VMEM((M + 8, NCH * NB), F32),
            pltpu.VMEM((1, NCH * NB), F32),
            pltpu.VMEM((M, NCH * NB), BF16),
            pltpu.VMEM((NCH * NB, M), BF16),
            pltpu.VMEM((CY, NB), F32),
            pltpu.VMEM((ROWS, NB), F32),
            pltpu.VMEM((M + 8, 128), F32),
            pltpu.VMEM((ROWS * CY, NCH * NB), BF16),
            pltpu.VMEM((ROWS, M, CY), F32),
            pltpu.VMEM((2, 2, LEV, M, CY), BF16),
            pltpu.VMEM((2, 2, LEV, M, CY), BF16),
            pltpu.VMEM((2, 2, M, CY), F32),
            pltpu.VMEM((2, 2, M, CY), F32),
            pltpu.SemaphoreType.DMA((NBLK, N_COPIES)),
            pltpu.SemaphoreType.DMA((NBLK, N_COPIES)),
            pltpu.SemaphoreType.DMA((N_FACES,)),
            pltpu.SemaphoreType.DMA((N_FACES,)),
        ],
        compiler_params=pltpu.CompilerParams(
            vmem_limit_bytes=VMEM_LIMIT, collective_id=0, has_side_effects=True
        ),
        name="filter",
    )(
        level_scale,
        channel_weights,
        error_var,
        owner_map,
        ensemble.reshape(M * ROWS, CY),
        observed,
        column_x,
        column_y,
        peak_level,
        courant_x.reshape(ROWS, CY),
        courant_y.reshape(ROWS, CY),
    )
    return result.reshape(ensemble.shape)


def solution(mesh):
    in_specs = (
        P(None, "lev", "gx", "gy"),
        P("lev"),
        P(None, "lev"),
        P(),
        P(),
        P(),
        P(),
        P(),
        P(),
        P("lev", "gx", "gy"),
        P("lev", "gx", "gy"),
    )
    out_specs = P(None, "lev", "gx", "gy")
    return jax.shard_map(shards, mesh=mesh, in_specs=in_specs, out_specs=out_specs, check_vma=False)
```

```python
import jax
import jax.numpy as jnp
from jax import lax
from jax.experimental import pallas as pl
from jax.experimental.pallas import tpu as pltpu
from jax.sharding import PartitionSpec as P

NB = 512
NCH = 4
NBLK = 2
PEAKW = 32
VLOC = 16
HLOC_X = 8
HLOC_Y = 512
KAPPA = 0.1

M = 96
LEV = 8
CX = 4
CY = 128
COLS = CX * CY
ROWS = LEV * CX
HALF = 256
GROUP = 4
LAST = 8
STEPS = M // ROWS * GROUP // 2
PIECE = 24
SOME = LEV // 2
N_FACES = 2 * (2 * 2 + 2 * 2)

F32 = jnp.float32
BF16 = jnp.bfloat16
HIGHEST = lax.Precision.HIGHEST
MESH = pl.DeviceIdType.MESH
VMEM_LIMIT = 56 * 1024 * 1024


def split3(value):
    high = value.astype(BF16)
    rest = value - high.astype(F32)
    middle = rest.astype(BF16)
    low = (rest - middle.astype(F32)).astype(BF16)
    return high, middle, low


def radiances(block, scale_ref, weight_ref, state, column_x_ref, column_y_ref, peak_ref, part, gathered):
    one = slice(block, block + 1)
    column = column_x_ref[one, :] * CY + column_y_ref[one, :]
    first_level = (lax.axis_index("lev") * LEV).astype(F32)
    chosen = (lax.broadcasted_iota(jnp.int32, (COLS, NB), 0) == column).astype(F32)
    chosen = chosen.astype(BF16)
    for level in range(LEV):
        profile = jnp.concatenate(
            [jnp.tanh(state[level * CX + x] * scale_ref[level]) for x in range(CX)], axis=1
        )
        parts = jnp.concatenate(split3(profile), axis=0)
        picked = jnp.dot(parts, chosen, preferred_element_type=F32)
        gathered[level] = picked[:M] + picked[M : 2 * M] + picked[2 * M :]
    peak = peak_ref[one, :].astype(F32)
    shapes = [
        jnp.exp(-jnp.square((first_level + level - peak) / PEAKW)) for level in range(LEV)
    ]

    def produce(channel):
        factors = [shapes[level] * weight_ref[channel, level] for level in range(LEV)]
        for tile in range(4):
            lanes = slice(tile * 128, tile * 128 + 128)
            half, quarter = tile // 2, tile % 2
            total = gathered[0, :, lanes] * factors[0][:, lanes]
            for level in range(1, LEV):
                total += gathered[level, :, lanes] * factors[level][:, lanes]
            part[half, channel, quarter * M : quarter * M + M, :] = total

    return produce


def row_of(kind, level, which):
    return level * CX + which * (3 - 2 * kind) + kind


def place():
    lev, gx, gy = lax.axis_index("lev"), lax.axis_index("gx"), lax.axis_index("gy")
    core, y = lax.rem(lev, 2), lax.div(lev, 2)
    x, z = lax.rem(gy, 4), gx * 2 + lax.div(gy, 4)

    def at(dx, dy, dz, dcore):
        there_x, there_y = lax.rem(x + dx, 4), lax.rem(y + dy, 4)
        there_z, there_core = lax.rem(z + dz, 8), lax.rem(core + dcore, 2)
        return (
            there_y * 2 + there_core,
            lax.div(there_z, 2),
            lax.rem(there_z, 2) * 4 + there_x,
        )

    beside = (
        (lev, lax.rem(gx + 1, 4), gy),
        (lev, lax.rem(gx + 3, 4), gy),
        (lev, gx, lax.rem(gy + 1, 8)),
        (lev, gx, lax.rem(gy + 7, 8)),
    )
    return x, y, z, core, at, beside


def share(block, produce, owner_ref, part, whole, from_core, sums, from_y, from_z, from_x, send, recv):
    x, y, z, core, at, _ = place()
    owner = owner_ref[block]
    owner_z = lax.div(owner, 8) * 2 + lax.div(lax.rem(owner, 8), 4)
    owner_x = lax.rem(owner, 4)
    y_at = lambda d: lax.rem(y + d, 4)
    z_at = lambda d: lax.rem(z + d, 8)
    to_core = at(0, 0, 0, 1)
    to_x = lambda d: at(d, 0, 0, 0)
    to_y = lambda d: at(0, d, 0, 0)
    to_z = lambda d: at(0, 0, d, 0)
    slot = [0]
    started = []

    def start(src, dst, device):
        number = slot[0]
        slot[0] += 1
        copy = pltpu.make_async_remote_copy(
            src_ref=src,
            dst_ref=dst,
            send_sem=send.at[block, number],
            recv_sem=recv.at[block, number],
            device_id=device,
            device_id_type=MESH,
        )
        copy.start()
        started.append(copy)
        return copy

    def arrive(copies):
        for copy in copies:
            copy.wait_recv()

    sent = []

    def pass_on(d, copy):
        copy.wait_recv()
        here = y_at(d)
        sums[here] = part[core, here] + from_core[here]
        if d > 0:
            sent.append(start(sums.at[here], from_y.at[d - 1], to_y(d)))

    before = None
    for d in (2, 1, 3, 0):
        produce(y_at(d))
        copy = start(part.at[1 - core, y_at(d)], from_core.at[y_at(d)], to_core)
        if before is not None:
            pass_on(*before)
        before = d, copy
    pass_on(*before)
    arrive(sent)
    sums[y] = sums[y] + from_y[0] + from_y[1] + from_y[2]

    far_first = (4, 3, 5, 2, 6, 1, 7)
    sent = [
        start(sums.at[y, pl.ds(z_at(d) * PIECE, PIECE)], from_z.at[z], to_z(d))
        for d in far_first
    ]
    mine = pl.ds(pl.multiple_of(z * PIECE, 8), PIECE)
    from_z[z] = sums[y, mine]
    arrive(sent)
    from_x[x] = from_z[owner_z]
    own = from_x.at[x]
    arrive([start(own, own, to_x(d)) for d in (2, 1, 3)])
    whole[core, y, mine] = from_x[owner_x]
    own = whole.at[core, y, mine]
    arrive([start(own, own, to_z(d)) for d in far_first])
    own = whole.at[core, y]
    sent = [start(own, own, to_y(d)) for d in (2, 1, 3)]
    flying = [start(own, own, to_core)]
    for d, copy in zip((2, 1, 3), sent):
        copy.wait_recv()
        came = whole.at[core, y_at(4 - d)]
        flying.append(start(came, came, to_core))
    arrive(flying)
    for copy in started:
        copy.wait_send()


N_COPIES = 4 + 3 + 7 + 3 + 7 + 3 + 4


def assimilate(
    block,
    owner_ref,
    error_ref,
    state,
    whole,
    observed_ref,
    column_x_ref,
    column_y_ref,
    peak_ref,
    spread,
    scaled,
    innovation,
    pert,
    solved_t,
    taper_y,
    taper_vx,
    system,
    weight,
    then,
):
    owner = owner_ref[block]
    one = slice(block, block + 1)
    inverses = [1.0 / jnp.full((1, 128), error_ref[channel], F32) for channel in range(NCH)]
    for channel in range(NCH):
        inverse = inverses[channel]
        for tile in range(4):
            half, quarter = tile // 2, tile % 2
            evolved = whole[half, channel, quarter * M : quarter * M + M, :]
            mean = jnp.sum(evolved, axis=0, keepdims=True) * (1.0 / M)
            lanes = slice(channel * NB + tile * 128, channel * NB + tile * 128 + 128)
            part = evolved - mean
            spread[:, lanes] = part
            pert[:, lanes] = part.astype(BF16)
            scaled[:M, lanes] = part * inverse
            away = observed_ref[block, channel : channel + 1, tile * 128 : tile * 128 + 128] - mean
            innovation[:, lanes] = away
            scaled[M:, lanes] = jnp.broadcast_to(away * inverse, (8, 128))
    cross = lax.dot_general(
        scaled[...], spread[...], (((1,), (1,)), ((), ())), precision=HIGHEST,
        preferred_element_type=F32,
    )
    lane = lax.broadcasted_iota(jnp.int32, (M + 8, 128), 1)
    row = lax.broadcasted_iota(jnp.int32, (M + 8, 128), 0)
    cross = jnp.concatenate([cross, jnp.zeros((M + 8, 128 - M), F32)], axis=1)
    system[...] = cross + jnp.where((lane == row) & (row < M), float(M - 1), 0.0)

    peak = peak_ref[one, :].astype(F32)
    at_x = lax.div(owner, 8) * CX + column_x_ref[one, :]
    at_y = lax.rem(owner, 8) * CY + column_y_ref[one, :]
    grid_y = lax.axis_index("gy") * CY + lax.broadcasted_iota(jnp.int32, (CY, NB), 0)
    gap = jnp.abs(grid_y - at_y)
    gap = jnp.minimum(gap, 8 * CY - gap).astype(F32)
    taper_y[...] = jnp.exp(-jnp.square(gap / HLOC_Y))
    index = lax.broadcasted_iota(jnp.int32, (ROWS, NB), 0)
    grid_x = lax.axis_index("gx") * CX + lax.rem(index, CX)
    gap = jnp.abs(grid_x - at_x)
    gap = jnp.minimum(gap, 4 * CX - gap).astype(F32)
    level = (lax.axis_index("lev") * LEV + lax.div(index, CX)).astype(F32)
    taper_vx[...] = (
        jnp.exp(-jnp.square((level - peak) / VLOC)) * jnp.exp(-jnp.square(gap / HLOC_X))
    ) * (1.0 / (M - 1))

    def sweep(pair):
        p, q = pair * 2, pair * 2 + 1
        matrix = system[...]
        row_p, row_q = system[pl.ds(p, 1), :], system[pl.ds(q, 1), :]
        at_p, at_q = jnp.full((M + 8, 128), p, jnp.int32), jnp.full((M + 8, 128), q, jnp.int32)
        column_p = jnp.take_along_axis(matrix, at_p, axis=1)
        column_q = jnp.take_along_axis(matrix, at_q, axis=1)
        rows_p, rows_q = jnp.broadcast_to(row_p, (8, 128)), jnp.broadcast_to(row_q, (8, 128))
        pp = jnp.take_along_axis(rows_p, at_p[:8], axis=1)[:1]
        pq = jnp.take_along_axis(rows_p, at_q[:8], axis=1)[:1]
        qq = jnp.take_along_axis(rows_q, at_q[:8], axis=1)[:1]
        inverse = 1.0 / (pp * qq - pq * pq)
        lane_p, lane_q = lane == p, lane == q
        away = lane_p[:1] | lane_q[:1]
        row_p = jnp.where(away, jnp.where(lane_p[:1], -1.0, 0.0), row_p)
        row_q = jnp.where(away, jnp.where(lane_q[:1], -1.0, 0.0), row_q)
        times_p = (qq * inverse) * row_p - (pq * inverse) * row_q
        times_q = (pp * inverse) * row_q - (pq * inverse) * row_p
        is_p, is_q = row == p, row == q
        swept = is_p | is_q
        column_p = jnp.where(swept, jnp.where(is_p, -1.0, 0.0), column_p)
        column_q = jnp.where(swept, jnp.where(is_q, -1.0, 0.0), column_q)
        matrix = jnp.where(swept | lane_p | lane_q, 0.0, matrix)
        system[...] = matrix - column_p * times_p - column_q * times_q

    @pl.loop(0, ROWS // GROUP)
    def _(group):
        for turn in range(STEPS):
            sweep(group * STEPS + turn)
        anomalies = []
        besides = []
        for at in range(GROUP):
            here = row_of(lax.div(group, 4), lax.rem(group, 4) * (GROUP // 2) + at // 2, at % 2)
            member = state[here]
            anomaly = member - jnp.sum(member, axis=0, keepdims=True) * (1.0 / M)
            anomalies.append(anomaly.T.astype(BF16))
            besides.append(taper_vx[pl.ds(here, 1), :])
        anomaly = jnp.concatenate(anomalies, axis=0)
        for chunk in range(NB // HALF):
            near = slice(chunk * HALF, chunk * HALF + HALF)
            taper = jnp.concatenate([taper_y[:, near] * b[:, near] for b in besides], axis=0)
            for channel in range(NCH):
                lanes = slice(channel * NB + chunk * HALF, channel * NB + chunk * HALF + HALF)
                covariance = jnp.dot(anomaly, pert[:, lanes], preferred_element_type=F32)
                rows = pl.ds(group * (GROUP * CY), GROUP * CY)
                weight[rows, lanes] = (taper * covariance).astype(BF16)

    swept = system[...]
    gain = (swept[M : M + 1] - 0.5 * (M - 1) * swept[:M])[:, :M]
    for channel in range(NCH):
        lanes = slice(channel * NB, channel * NB + NB)
        change = jnp.dot(gain, spread[:, lanes], precision=HIGHEST, preferred_element_type=F32)
        solved = inverses[channel][:, :1] * (innovation[:, lanes] - change)
        solved_t[lanes, :] = solved.T.astype(BF16)

    def finish(group):
        update = jnp.dot(
            weight[pl.ds(group * (LAST * CY), LAST * CY), :],
            solved_t[...],
            preferred_element_type=F32,
        )
        for at in range(LAST):
            here = row_of(group // 2, group % 2 * (LAST // 2) + at // 2, at % 2)
            state[here] = state[here] + update[at * CY : at * CY + CY].T

    for group in range(ROWS // LAST):
        finish(group)
        if then is not None:
            then(group)


def transport(speed_x_ref, speed_y_ref, state, out_ref, middle, face, got, edge, came, send, recv):
    targets = place()[-1]
    lane = lax.broadcasted_iota(jnp.int32, (M, CY), 1)
    copies = {}

    def start(key, src, dst, target):
        number = len(copies)
        copies[key] = pltpu.make_async_remote_copy(
            src_ref=src,
            dst_ref=dst,
            send_sem=send.at[number],
            recv_sem=recv.at[number],
            device_id=target,
            device_id_type=MESH,
        )
        copies[key].start()

    def send_faces(turn, half):
        source = middle if turn else state
        for level in range(half * SOME, half * SOME + SOME):
            face[turn, 0, level] = source[level * CX + CX - 1].astype(BF16)
            face[turn, 1, level] = source[level * CX].astype(BF16)
        some = pl.ds(half * SOME, SOME)
        for n in range(2):
            start(("x", turn, half, n), face.at[turn, n, some], got.at[turn, n, some], targets[n])

    def send_edges(turn, kind):
        source = middle if turn else state

        def pack(level, packed):
            for which in range(2):
                slot = level * 2 + which
                turned = pltpu.roll(source[row_of(kind, level, which)], slot * 2 + 2, 1)
                here = (lane == slot * 2 + 1) | (lane == slot * 2 + 2)
                packed = jnp.where(here, turned, packed)
            return packed

        edge[turn, kind] = lax.fori_loop(0, LEV, pack, jnp.zeros((M, CY), F32))
        for n in range(2):
            start(
                ("y", turn, kind, n), edge.at[turn, kind], came.at[turn, kind, n], targets[2 + n]
            )

    def take_edges(turn, kind):
        for n in range(2):
            copies["y", turn, kind, n].wait_recv()
        return jnp.where(
            lax.rem(lane, 2) == 1,
            came[turn, kind, 0],
            pltpu.roll(came[turn, kind, 1], CY - 2, 1),
        )

    def advance(turn, kind, edges, level):
        source = middle if turn else state
        for which in range(2):
            at = row_of(kind, level, which)
            centre = source[at]
            if kind == 0 and which == 0:
                west = got[turn, 0, level].astype(F32)
            else:
                west = source[at - 1]
            if kind == 0 and which == 1:
                east = got[turn, 1, level].astype(F32)
            else:
                east = source[at + 1]
            beyond = pltpu.roll(edges, CY - 1 - 2 * (level * 2 + which), 1)
            south = jnp.where(lane == 0, beyond, pltpu.roll(centre, 1, 1))
            north = jnp.where(lane == CY - 1, beyond, pltpu.roll(centre, CY - 1, 1))
            u = speed_x_ref[pl.ds(at, 1), :]
            v = speed_y_ref[pl.ds(at, 1), :]
            value = (
                centre * (1.0 - 4.0 * KAPPA - jnp.abs(u) - jnp.abs(v))
                + west * (jnp.maximum(u, 0.0) + KAPPA)
                + east * (KAPPA - jnp.minimum(u, 0.0))
                + south * (jnp.maximum(v, 0.0) + KAPPA)
                + north * (KAPPA - jnp.minimum(v, 0.0))
            )
            if turn == 0:
                middle[at] = value
            else:
                out_ref[pl.ds(at, M, stride=ROWS), :] = value

    def levels(turn, kind, edges, first, last):
        pl.loop(first, last)(lambda level: advance(turn, kind, edges, level))

    def outer(turn):
        edges = take_edges(turn, 0)
        for half in range(LEV // SOME):
            for n in range(2):
                copies["x", turn, half, n].wait_recv()
            levels(turn, 0, edges, half * SOME, half * SOME + SOME)
            if turn == 0:
                send_faces(1, half)

    def inner(turn):
        levels(turn, 1, take_edges(turn, 1), 0, LEV)

    def early(group):
        if group < 2:
            send_faces(0, group)
        if group == 1:
            send_edges(0, 0)
        if group == 3:
            send_edges(0, 1)

    def rest():
        outer(0)
        send_edges(1, 0)
        inner(0)
        send_edges(1, 1)
        inner(1)
        outer(1)
        for copy in copies.values():
            copy.wait_send()

    return early, rest


def filter_kernel(
    scale_ref,
    weight_ref,
    error_ref,
    owner_ref,
    ensemble_ref,
    observed_ref,
    column_x_ref,
    column_y_ref,
    peak_ref,
    speed_x_ref,
    speed_y_ref,
    out_ref,
    state,
    gathered,
    part,
    whole_0,
    whole_1,
    from_core_0,
    from_core_1,
    sums,
    from_y_0,
    from_y_1,
    from_z_0,
    from_z_1,
    from_x_0,
    from_x_1,
    spread,
    scaled,
    innovation,
    pert,
    solved_t,
    taper_y,
    taper_vx,
    system,
    weight,
    middle,
    face,
    got,
    edge,
    came,
    send,
    recv,
    face_send,
    face_recv,
):
    at, beside = place()[-2:]
    peers = [at(0, 0, 0, 1)] + [at(0, d, 0, 0) for d in range(1, 4)]
    peers += [at(0, 0, d, 0) for d in range(1, 8)] + [at(d, 0, 0, 0) for d in range(1, 4)]
    peers += beside
    barrier = pltpu.get_barrier_semaphore()
    for peer in peers:
        pl.semaphore_signal(barrier, inc=1, device_id=peer, device_id_type=MESH)

    for row in range(ROWS):
        state[row] = ensemble_ref[pl.ds(row, M, stride=ROWS), :]
    early, rest = transport(
        speed_x_ref, speed_y_ref, state, out_ref, middle, face, got, edge, came, face_send,
        face_recv,
    )
    for block in range(NBLK):
        produce = radiances(
            block, scale_ref, weight_ref, state, column_x_ref, column_y_ref, peak_ref, part,
            gathered,
        )
        if block == 0:
            pl.semaphore_wait(barrier, len(peers))
        whole = (whole_0, whole_1)[block]
        from_core = (from_core_0, from_core_1)[block]
        from_y = (from_y_0, from_y_1)[block]
        from_z = (from_z_0, from_z_1)[block]
        from_x = (from_x_0, from_x_1)[block]
        share(
            block, produce, owner_ref, part, whole, from_core, sums, from_y, from_z, from_x, send,
            recv,
        )
        then = None if block < NBLK - 1 else early
        assimilate(
            block, owner_ref, error_ref, state, whole, observed_ref, column_x_ref, column_y_ref,
            peak_ref, spread, scaled, innovation, pert, solved_t, taper_y, taper_vx, system, weight,
            then,
        )
    rest()


SMEM_SPEC = pl.BlockSpec(memory_space=pltpu.SMEM)
VMEM_SPEC = pl.BlockSpec(memory_space=pltpu.VMEM)


def shards(
    ensemble,
    level_scale,
    channel_weights,
    error_var,
    observed,
    column_x,
    column_y,
    peak_level,
    owner_map,
    courant_x,
    courant_y,
):
    result = pl.pallas_call(
        filter_kernel,
        out_shape=jax.ShapeDtypeStruct((M * ROWS, CY), F32),
        in_specs=[SMEM_SPEC] * 4 + [VMEM_SPEC] * 7,
        out_specs=VMEM_SPEC,
        scratch_shapes=[
            pltpu.VMEM((ROWS, M, CY), F32),
            pltpu.VMEM((LEV, M, NB), F32),
            pltpu.VMEM((2, NCH, 2 * M, 128), F32),
            *[pltpu.VMEM((2, NCH, 2 * M, 128), F32)] * NBLK,
            *[pltpu.VMEM((4, 2 * M, 128), F32)] * NBLK,
            pltpu.VMEM((4, 2 * M, 128), F32),
            *[pltpu.VMEM((3, 2 * M, 128), F32)] * NBLK,
            *[pltpu.VMEM((8, PIECE, 128), F32)] * NBLK,
            *[pltpu.VMEM((4, PIECE, 128), F32)] * NBLK,
            pltpu.VMEM((M, NCH * NB), F32),
            pltpu.VMEM((M + 8, NCH * NB), F32),
            pltpu.VMEM((1, NCH * NB), F32),
            pltpu.VMEM((M, NCH * NB), BF16),
            pltpu.VMEM((NCH * NB, M), BF16),
            pltpu.VMEM((CY, NB), F32),
            pltpu.VMEM((ROWS, NB), F32),
            pltpu.VMEM((M + 8, 128), F32),
            pltpu.VMEM((ROWS * CY, NCH * NB), BF16),
            pltpu.VMEM((ROWS, M, CY), F32),
            pltpu.VMEM((2, 2, LEV, M, CY), BF16),
            pltpu.VMEM((2, 2, LEV, M, CY), BF16),
            pltpu.VMEM((2, 2, M, CY), F32),
            pltpu.VMEM((2, 2, 2, M, CY), F32),
            pltpu.SemaphoreType.DMA((NBLK, N_COPIES)),
            pltpu.SemaphoreType.DMA((NBLK, N_COPIES)),
            pltpu.SemaphoreType.DMA((N_FACES,)),
            pltpu.SemaphoreType.DMA((N_FACES,)),
        ],
        compiler_params=pltpu.CompilerParams(
            vmem_limit_bytes=VMEM_LIMIT, collective_id=0, has_side_effects=True
        ),
        name="filter",
    )(
        level_scale,
        channel_weights,
        error_var,
        owner_map,
        ensemble.reshape(M * ROWS, CY),
        observed,
        column_x,
        column_y,
        peak_level,
        courant_x.reshape(ROWS, CY),
        courant_y.reshape(ROWS, CY),
    )
    return result.reshape(ensemble.shape)


def solution(mesh):
    in_specs = (
        P(None, "lev", "gx", "gy"),
        P("lev"),
        P(None, "lev"),
        P(),
        P(),
        P(),
        P(),
        P(),
        P(),
        P("lev", "gx", "gy"),
        P("lev", "gx", "gy"),
    )
    out_specs = P(None, "lev", "gx", "gy")
    return jax.shard_map(shards, mesh=mesh, in_specs=in_specs, out_specs=out_specs, check_vma=False)
```

```python
import jax
import jax.numpy as jnp
from jax import lax
from jax.experimental import pallas as pl
from jax.experimental.pallas import tpu as pltpu
from jax.sharding import PartitionSpec as P

NB = 512
NCH = 4
NBLK = 2
PEAKW = 32
VLOC = 16
HLOC_X = 8
HLOC_Y = 512
KAPPA = 0.1

M = 96
LEV = 8
CX = 4
CY = 128
COLS = CX * CY
ROWS = LEV * CX
HALF = 256
GROUP = 4
LAST = 8
STEPS = M // ROWS * GROUP // 2
PIECE = 24
SOME = LEV // 2
N_FACES = 2 * (2 * 2 + 2 * 2)

F32 = jnp.float32
BF16 = jnp.bfloat16
HIGHEST = lax.Precision.HIGHEST
MESH = pl.DeviceIdType.MESH
VMEM_LIMIT = 56 * 1024 * 1024


def split3(value):
    high = value.astype(BF16)
    rest = value - high.astype(F32)
    middle = rest.astype(BF16)
    low = (rest - middle.astype(F32)).astype(BF16)
    return high, middle, low


def radiances(block, scale_ref, weight_ref, state, column_x_ref, column_y_ref, peak_ref, part, gathered):
    one = slice(block, block + 1)
    column = column_x_ref[one, :] * CY + column_y_ref[one, :]
    first_level = (lax.axis_index("lev") * LEV).astype(F32)
    chosen = (lax.broadcasted_iota(jnp.int32, (COLS, NB), 0) == column).astype(F32)
    chosen = chosen.astype(BF16)
    for level in range(LEV):
        profile = jnp.concatenate(
            [jnp.tanh(state[level * CX + x] * scale_ref[level]) for x in range(CX)], axis=1
        )
        parts = jnp.concatenate(split3(profile), axis=0)
        picked = jnp.dot(parts, chosen, preferred_element_type=F32)
        gathered[level] = picked[:M] + picked[M : 2 * M] + picked[2 * M :]
    peak = peak_ref[one, :].astype(F32)
    shapes = [
        jnp.exp(-jnp.square((first_level + level - peak) / PEAKW)) for level in range(LEV)
    ]

    def produce(channel):
        factors = [shapes[level] * weight_ref[channel, level] for level in range(LEV)]
        for tile in range(4):
            lanes = slice(tile * 128, tile * 128 + 128)
            half, quarter = tile // 2, tile % 2
            total = gathered[0, :, lanes] * factors[0][:, lanes]
            for level in range(1, LEV):
                total += gathered[level, :, lanes] * factors[level][:, lanes]
            part[half, channel, quarter * M : quarter * M + M, :] = total

    return produce


def row_of(kind, level, which):
    return level * CX + which * (3 - 2 * kind) + kind


def place():
    lev, gx, gy = lax.axis_index("lev"), lax.axis_index("gx"), lax.axis_index("gy")
    core, y = lax.rem(lev, 2), lax.div(lev, 2)
    x, z = lax.rem(gy, 4), gx * 2 + lax.div(gy, 4)

    def at(dx, dy, dz, dcore):
        there_x, there_y = lax.rem(x + dx, 4), lax.rem(y + dy, 4)
        there_z, there_core = lax.rem(z + dz, 8), lax.rem(core + dcore, 2)
        return (
            there_y * 2 + there_core,
            lax.div(there_z, 2),
            lax.rem(there_z, 2) * 4 + there_x,
        )

    beside = (
        (lev, lax.rem(gx + 1, 4), gy),
        (lev, lax.rem(gx + 3, 4), gy),
        (lev, gx, lax.rem(gy + 1, 8)),
        (lev, gx, lax.rem(gy + 7, 8)),
    )
    return x, y, z, core, at, beside


def share(block, enter, produce, meanwhile, digest, owner_ref, part, whole, from_core, sums, from_y, from_z, from_x, send, recv):
    x, y, z, core, at, _ = place()
    owner = owner_ref[block]
    owner_z = lax.div(owner, 8) * 2 + lax.div(lax.rem(owner, 8), 4)
    owner_x = lax.rem(owner, 4)
    y_at = lambda d: lax.rem(y + d, 4)
    z_at = lambda d: lax.rem(z + d, 8)
    to_core = at(0, 0, 0, 1)
    to_x = lambda d: at(d, 0, 0, 0)
    to_y = lambda d: at(0, d, 0, 0)
    to_z = lambda d: at(0, 0, d, 0)
    slot = [0]
    started = []

    def start(src, dst, device):
        number = slot[0]
        slot[0] += 1
        copy = pltpu.make_async_remote_copy(
            src_ref=src,
            dst_ref=dst,
            send_sem=send.at[block, number],
            recv_sem=recv.at[block, number],
            device_id=device,
            device_id_type=MESH,
        )
        copy.start()
        started.append(copy)
        return copy

    def arrive(copies):
        for copy in copies:
            copy.wait_recv()

    sent = []

    def pass_on(d, copy):
        copy.wait_recv()
        here = y_at(d)
        sums[here] = part[core, here] + from_core[here]
        if d > 0:
            sent.append(start(sums.at[here], from_y.at[d - 1], to_y(d)))

    before = None
    order = (2, 1, 3, 0)
    if enter is not None:
        for d in order:
            produce(y_at(d))
        meanwhile()
        enter()
    for d in order:
        if enter is None:
            produce(y_at(d))
        copy = start(part.at[1 - core, y_at(d)], from_core.at[y_at(d)], to_core)
        if before is not None:
            pass_on(*before)
        before = d, copy
    pass_on(*before)
    arrive(sent)
    sums[y] = sums[y] + from_y[0] + from_y[1] + from_y[2]

    far_first = (4, 3, 5, 2, 6, 1, 7)
    sent = [
        start(sums.at[y, pl.ds(z_at(d) * PIECE, PIECE)], from_z.at[z], to_z(d))
        for d in far_first
    ]
    mine = pl.ds(pl.multiple_of(z * PIECE, 8), PIECE)
    from_z[z] = sums[y, mine]
    if enter is None:
        meanwhile()
    arrive(sent)
    from_x[x] = from_z[owner_z]
    own = from_x.at[x]
    arrive([start(own, own, to_x(d)) for d in (2, 1, 3)])
    whole[core, y, mine] = from_x[owner_x]
    own = whole.at[core, y, mine]
    arrive([start(own, own, to_z(d)) for d in far_first])
    own = whole.at[core, y]
    sent = {d: start(own, own, to_y(d)) for d in (2, 1, 3)}
    before = start(own, own, to_core), y
    for d in (1, 3, 2):
        sent[d].wait_recv()
        came = whole.at[core, y_at(4 - d)]
        after = start(came, came, to_core), y_at(4 - d)
        before[0].wait_recv()
        digest(before[1])
        before = after
    before[0].wait_recv()
    digest(before[1])
    return started


N_COPIES = 4 + 3 + 7 + 3 + 7 + 3 + 4


def assimilate(
    block,
    owner_ref,
    error_ref,
    state,
    whole,
    observed_ref,
    column_x_ref,
    column_y_ref,
    peak_ref,
    spread,
    scaled,
    innovation,
    pert,
    solved_t,
    taper_y,
    taper_vx,
    system,
    weight,
    share_now,
    then,
):
    owner = owner_ref[block]
    one = slice(block, block + 1)
    cross = []

    def inverse_of(channel):
        return 1.0 / jnp.full((1, 128), error_ref[channel], F32)

    def digest(channel):
        inverse = inverse_of(channel)
        this = lax.broadcasted_iota(jnp.int32, (NCH, 128), 0) == channel
        for tile in range(4):
            half, quarter = tile // 2, tile % 2
            evolved = whole[half, channel, quarter * M : quarter * M + M, :]
            mean = jnp.sum(evolved, axis=0, keepdims=True) * (1.0 / M)
            lanes = slice(tile * 128, tile * 128 + 128)
            part = evolved - mean
            spread[channel, :, lanes] = part
            pert[channel, :, lanes] = part.astype(BF16)
            scaled[:M, lanes] = part * inverse
            wanted = jnp.where(this, observed_ref[block, :, lanes], 0.0)
            away = jnp.sum(wanted, axis=0, keepdims=True) - mean
            innovation[channel, :, lanes] = away
            scaled[M:, lanes] = jnp.broadcast_to(away * inverse, (8, 128))
        cross.append(
            lax.dot_general(
                scaled[...], spread[channel], (((1,), (1,)), ((), ())), precision=HIGHEST,
                preferred_element_type=F32,
            )
        )

    def tapers():
        peak = peak_ref[one, :].astype(F32)
        at_x = lax.div(owner, 8) * CX + column_x_ref[one, :]
        at_y = lax.rem(owner, 8) * CY + column_y_ref[one, :]
        grid_y = lax.axis_index("gy") * CY + lax.broadcasted_iota(jnp.int32, (CY, NB), 0)
        gap = jnp.abs(grid_y - at_y)
        gap = jnp.minimum(gap, 8 * CY - gap).astype(F32)
        taper_y[...] = jnp.exp(-jnp.square(gap / HLOC_Y))
        index = lax.broadcasted_iota(jnp.int32, (ROWS, NB), 0)
        grid_x = lax.axis_index("gx") * CX + lax.rem(index, CX)
        gap = jnp.abs(grid_x - at_x)
        gap = jnp.minimum(gap, 4 * CX - gap).astype(F32)
        level = (lax.axis_index("lev") * LEV + lax.div(index, CX)).astype(F32)
        taper_vx[...] = (
            jnp.exp(-jnp.square((level - peak) / VLOC)) * jnp.exp(-jnp.square(gap / HLOC_X))
        ) * (1.0 / (M - 1))

    started = share_now(tapers, digest)
    cross = cross[0] + cross[1] + cross[2] + cross[3]
    lane = lax.broadcasted_iota(jnp.int32, (M + 8, 128), 1)
    row = lax.broadcasted_iota(jnp.int32, (M + 8, 128), 0)
    cross = jnp.concatenate([cross, jnp.zeros((M + 8, 128 - M), F32)], axis=1)
    system[...] = cross + jnp.where((lane == row) & (row < M), float(M - 1), 0.0)

    def sweep(pair):
        p, q = pair * 2, pair * 2 + 1
        matrix = system[...]
        row_p, row_q = system[pl.ds(p, 1), :], system[pl.ds(q, 1), :]
        at_p, at_q = jnp.full((M + 8, 128), p, jnp.int32), jnp.full((M + 8, 128), q, jnp.int32)
        column_p = jnp.take_along_axis(matrix, at_p, axis=1)
        column_q = jnp.take_along_axis(matrix, at_q, axis=1)
        rows_p, rows_q = jnp.broadcast_to(row_p, (8, 128)), jnp.broadcast_to(row_q, (8, 128))
        pp = jnp.take_along_axis(rows_p, at_p[:8], axis=1)[:1]
        pq = jnp.take_along_axis(rows_p, at_q[:8], axis=1)[:1]
        qq = jnp.take_along_axis(rows_q, at_q[:8], axis=1)[:1]
        inverse = 1.0 / (pp * qq - pq * pq)
        lane_p, lane_q = lane == p, lane == q
        away = lane_p[:1] | lane_q[:1]
        row_p = jnp.where(away, jnp.where(lane_p[:1], -1.0, 0.0), row_p)
        row_q = jnp.where(away, jnp.where(lane_q[:1], -1.0, 0.0), row_q)
        times_p = (qq * inverse) * row_p - (pq * inverse) * row_q
        times_q = (pp * inverse) * row_q - (pq * inverse) * row_p
        is_p, is_q = row == p, row == q
        swept = is_p | is_q
        column_p = jnp.where(swept, jnp.where(is_p, -1.0, 0.0), column_p)
        column_q = jnp.where(swept, jnp.where(is_q, -1.0, 0.0), column_q)
        matrix = jnp.where(swept | lane_p | lane_q, 0.0, matrix)
        system[...] = matrix - column_p * times_p - column_q * times_q

    @pl.loop(0, ROWS // GROUP)
    def _(group):
        for turn in range(STEPS):
            sweep(group * STEPS + turn)
        anomalies = []
        besides = []
        for at in range(GROUP):
            here = row_of(lax.div(group, 4), lax.rem(group, 4) * (GROUP // 2) + at // 2, at % 2)
            member = state[here]
            anomaly = member - jnp.sum(member, axis=0, keepdims=True) * (1.0 / M)
            anomalies.append(anomaly.T.astype(BF16))
            besides.append(taper_vx[pl.ds(here, 1), :])
        anomaly = jnp.concatenate(anomalies, axis=0)
        for chunk in range(NB // HALF):
            near = slice(chunk * HALF, chunk * HALF + HALF)
            taper = jnp.concatenate([taper_y[:, near] * b[:, near] for b in besides], axis=0)
            for channel in range(NCH):
                lanes = slice(channel * NB + chunk * HALF, channel * NB + chunk * HALF + HALF)
                covariance = jnp.dot(
                    anomaly, pert[channel, :, near], preferred_element_type=F32
                )
                rows = pl.ds(group * (GROUP * CY), GROUP * CY)
                weight[rows, lanes] = (taper * covariance).astype(BF16)

    swept = system[...]
    gain = (swept[M : M + 1] - 0.5 * (M - 1) * swept[:M])[:, :M]
    for channel in range(NCH):
        lanes = slice(channel * NB, channel * NB + NB)
        change = jnp.dot(gain, spread[channel], precision=HIGHEST, preferred_element_type=F32)
        solved = inverse_of(channel)[:, :1] * (innovation[channel] - change)
        solved_t[lanes, :] = solved.T.astype(BF16)

    def finish(group):
        update = jnp.dot(
            weight[pl.ds(group * (LAST * CY), LAST * CY), :],
            solved_t[...],
            preferred_element_type=F32,
        )
        for at in range(LAST):
            here = row_of(group // 2, group % 2 * (LAST // 2) + at // 2, at % 2)
            state[here] = state[here] + update[at * CY : at * CY + CY].T

    for group in range(ROWS // LAST):
        finish(group)
        if then is not None:
            then(group)
    for copy in started:
        copy.wait_send()


def transport(speed_x_ref, speed_y_ref, state, out_ref, middle, face, got, edge, came, send, recv):
    targets = place()[-1]
    lane = lax.broadcasted_iota(jnp.int32, (M, CY), 1)
    copies = {}

    def start(key, src, dst, target):
        number = len(copies)
        copies[key] = pltpu.make_async_remote_copy(
            src_ref=src,
            dst_ref=dst,
            send_sem=send.at[number],
            recv_sem=recv.at[number],
            device_id=target,
            device_id_type=MESH,
        )
        copies[key].start()

    def send_faces(turn, half):
        source = middle if turn else state
        for level in range(half * SOME, half * SOME + SOME):
            face[turn, 0, level] = source[level * CX + CX - 1].astype(BF16)
            face[turn, 1, level] = source[level * CX].astype(BF16)
        some = pl.ds(half * SOME, SOME)
        for n in range(2):
            start(("x", turn, half, n), face.at[turn, n, some], got.at[turn, n, some], targets[n])

    def send_edges(turn, kind):
        source = middle if turn else state

        def pack(level, packed):
            for which in range(2):
                slot = level * 2 + which
                turned = pltpu.roll(source[row_of(kind, level, which)], slot * 2 + 2, 1)
                here = (lane == slot * 2 + 1) | (lane == slot * 2 + 2)
                packed = jnp.where(here, turned, packed)
            return packed

        edge[turn, kind] = lax.fori_loop(0, LEV, pack, jnp.zeros((M, CY), F32))
        for n in range(2):
            start(
                ("y", turn, kind, n), edge.at[turn, kind], came.at[turn, kind, n], targets[2 + n]
            )

    def take_edges(turn, kind):
        for n in range(2):
            copies["y", turn, kind, n].wait_recv()
        return jnp.where(
            lax.rem(lane, 2) == 1,
            came[turn, kind, 0],
            pltpu.roll(came[turn, kind, 1], CY - 2, 1),
        )

    def advance(turn, kind, edges, level):
        source = middle if turn else state
        for which in range(2):
            at = row_of(kind, level, which)
            centre = source[at]
            u = speed_x_ref[pl.ds(at, 1), :]
            v = speed_y_ref[pl.ds(at, 1), :]
            value = centre * (1.0 - 4.0 * KAPPA - jnp.abs(u) - jnp.abs(v))
            if kind == 1 or which == 1:
                value += source[at - 1] * (jnp.maximum(u, 0.0) + KAPPA)
            if kind == 1 or which == 0:
                value += source[at + 1] * (KAPPA - jnp.minimum(u, 0.0))
            beyond = pltpu.roll(edges, CY - 1 - 2 * (level * 2 + which), 1)
            south = jnp.where(lane == 0, beyond, pltpu.roll(centre, 1, 1))
            north = jnp.where(lane == CY - 1, beyond, pltpu.roll(centre, CY - 1, 1))
            value += south * (jnp.maximum(v, 0.0) + KAPPA) + north * (KAPPA - jnp.minimum(v, 0.0))
            if turn == 0:
                middle[at] = value
            elif kind == 0:
                state[at] = value
            else:
                out_ref[pl.ds(at, M, stride=ROWS), :] = value

    def complete(turn, level):
        for which in range(2):
            at = row_of(0, level, which)
            u = speed_x_ref[pl.ds(at, 1), :]
            factor = KAPPA - jnp.minimum(u, 0.0) if which else jnp.maximum(u, 0.0) + KAPPA
            term = got[turn, which, level].astype(F32) * factor
            if turn == 0:
                middle[at] = middle[at] + term
            else:
                out_ref[pl.ds(at, M, stride=ROWS), :] = state[at] + term

    def alone(turn, kind):
        edges = take_edges(turn, kind)
        pl.loop(0, LEV)(lambda level: advance(turn, kind, edges, level))

    def outer(turn):
        for half in range(LEV // SOME):
            for n in range(2):
                copies["x", turn, half, n].wait_recv()
            pl.loop(half * SOME, half * SOME + SOME)(lambda level: complete(turn, level))
            if turn == 0:
                send_faces(1, half)

    def early(group):
        if group < 2:
            send_faces(0, group)
        if group == 1:
            send_edges(0, 0)
        if group == 3:
            send_edges(0, 1)

    def rest():
        alone(0, 0)
        outer(0)
        send_edges(1, 0)
        alone(0, 1)
        send_edges(1, 1)
        alone(1, 0)
        alone(1, 1)
        outer(1)
        for copy in copies.values():
            copy.wait_send()

    return early, rest


def filter_kernel(
    scale_ref,
    weight_ref,
    error_ref,
    owner_ref,
    ensemble_ref,
    observed_ref,
    column_x_ref,
    column_y_ref,
    peak_ref,
    speed_x_ref,
    speed_y_ref,
    out_ref,
    state,
    gathered,
    part,
    whole_0,
    whole_1,
    from_core_0,
    from_core_1,
    sums,
    from_y_0,
    from_y_1,
    from_z_0,
    from_z_1,
    from_x_0,
    from_x_1,
    spread,
    scaled,
    innovation,
    pert,
    solved_t,
    taper_y,
    taper_vx,
    system,
    weight,
    middle,
    face,
    got,
    edge,
    came,
    send,
    recv,
    face_send,
    face_recv,
    landed,
    load_sem,
):
    load = pltpu.make_async_copy(ensemble_ref, landed, load_sem)
    load.start()
    at, beside = place()[-2:]
    peers = [at(0, 0, 0, 1)] + [at(0, d, 0, 0) for d in range(1, 4)]
    peers += [at(0, 0, d, 0) for d in range(1, 8)] + [at(d, 0, 0, 0) for d in range(1, 4)]
    peers += beside
    barrier = pltpu.get_barrier_semaphore()
    for peer in peers:
        pl.semaphore_signal(barrier, inc=1, device_id=peer, device_id_type=MESH)

    load.wait()
    for row in range(ROWS):
        state[row] = landed[pl.ds(row, M, stride=ROWS), :]

    def enter():
        pl.semaphore_wait(barrier, len(peers))

    early, rest = transport(
        speed_x_ref, speed_y_ref, state, out_ref, middle, face, got, edge, came, face_send,
        face_recv,
    )
    for block in range(NBLK):
        produce = radiances(
            block, scale_ref, weight_ref, state, column_x_ref, column_y_ref, peak_ref, part,
            gathered,
        )
        whole = (whole_0, whole_1)[block]
        from_core = (from_core_0, from_core_1)[block]
        from_y = (from_y_0, from_y_1)[block]
        from_z = (from_z_0, from_z_1)[block]
        from_x = (from_x_0, from_x_1)[block]

        def share_now(meanwhile, digest):
            return share(
                block, enter if block == 0 else None, produce, meanwhile, digest, owner_ref, part, whole, from_core, sums, from_y,
                from_z, from_x, send, recv,
            )

        then = None if block < NBLK - 1 else early
        assimilate(
            block, owner_ref, error_ref, state, whole, observed_ref, column_x_ref, column_y_ref,
            peak_ref, spread, scaled, innovation, pert, solved_t, taper_y, taper_vx, system, weight,
            share_now, then,
        )
    rest()


SMEM_SPEC = pl.BlockSpec(memory_space=pltpu.SMEM)
VMEM_SPEC = pl.BlockSpec(memory_space=pltpu.VMEM)


def shards(
    ensemble,
    level_scale,
    channel_weights,
    error_var,
    observed,
    column_x,
    column_y,
    peak_level,
    owner_map,
    courant_x,
    courant_y,
):
    result = pl.pallas_call(
        filter_kernel,
        out_shape=jax.ShapeDtypeStruct((M * ROWS, CY), F32),
        in_specs=[SMEM_SPEC] * 4 + [pl.BlockSpec(memory_space=pl.ANY)] + [VMEM_SPEC] * 6,
        out_specs=VMEM_SPEC,
        scratch_shapes=[
            pltpu.VMEM((ROWS, M, CY), F32),
            pltpu.VMEM((LEV, M, NB), F32),
            pltpu.VMEM((2, NCH, 2 * M, 128), F32),
            *[pltpu.VMEM((2, NCH, 2 * M, 128), F32)] * NBLK,
            *[pltpu.VMEM((4, 2 * M, 128), F32)] * NBLK,
            pltpu.VMEM((4, 2 * M, 128), F32),
            *[pltpu.VMEM((3, 2 * M, 128), F32)] * NBLK,
            *[pltpu.VMEM((8, PIECE, 128), F32)] * NBLK,
            *[pltpu.VMEM((4, PIECE, 128), F32)] * NBLK,
            pltpu.VMEM((NCH, M, NB), F32),
            pltpu.VMEM((M + 8, NB), F32),
            pltpu.VMEM((NCH, 1, NB), F32),
            pltpu.VMEM((NCH, M, NB), BF16),
            pltpu.VMEM((NCH * NB, M), BF16),
            pltpu.VMEM((CY, NB), F32),
            pltpu.VMEM((ROWS, NB), F32),
            pltpu.VMEM((M + 8, 128), F32),
            pltpu.VMEM((ROWS * CY, NCH * NB), BF16),
            pltpu.VMEM((ROWS, M, CY), F32),
            pltpu.VMEM((2, 2, LEV, M, CY), BF16),
            pltpu.VMEM((2, 2, LEV, M, CY), BF16),
            pltpu.VMEM((2, 2, M, CY), F32),
            pltpu.VMEM((2, 2, 2, M, CY), F32),
            pltpu.SemaphoreType.DMA((NBLK, N_COPIES)),
            pltpu.SemaphoreType.DMA((NBLK, N_COPIES)),
            pltpu.SemaphoreType.DMA((N_FACES,)),
            pltpu.SemaphoreType.DMA((N_FACES,)),
            pltpu.VMEM((M * ROWS, CY), F32),
            pltpu.SemaphoreType.DMA,
        ],
        compiler_params=pltpu.CompilerParams(
            vmem_limit_bytes=VMEM_LIMIT, collective_id=0, has_side_effects=True
        ),
        name="filter",
    )(
        level_scale,
        channel_weights,
        error_var,
        owner_map,
        ensemble.reshape(M * ROWS, CY),
        observed,
        column_x,
        column_y,
        peak_level,
        courant_x.reshape(ROWS, CY),
        courant_y.reshape(ROWS, CY),
    )
    return result.reshape(ensemble.shape)


def solution(mesh):
    in_specs = (
        P(None, "lev", "gx", "gy"),
        P("lev"),
        P(None, "lev"),
        P(),
        P(),
        P(),
        P(),
        P(),
        P(),
        P("lev", "gx", "gy"),
        P("lev", "gx", "gy"),
    )
    out_specs = P(None, "lev", "gx", "gy")
    return jax.shard_map(shards, mesh=mesh, in_specs=in_specs, out_specs=out_specs, check_vma=False)
```

```python
import jax
import jax.numpy as jnp
from jax import lax
from jax.experimental import pallas as pl
from jax.experimental.pallas import tpu as pltpu
from jax.sharding import PartitionSpec as P

NB = 512
NCH = 4
NBLK = 2
PEAKW = 32
VLOC = 16
HLOC_X = 8
HLOC_Y = 512
KAPPA = 0.1

M = 96
LEV = 8
CX = 4
CY = 128
COLS = CX * CY
ROWS = LEV * CX
HALF = 256
GROUP = 4
LAST = 8
STEPS = M // ROWS * GROUP // 2
PIECE = 24
SOME = LEV // 2
N_FACES = 2 * (2 * 2 + 2 * 2)

F32 = jnp.float32
BF16 = jnp.bfloat16
HIGHEST = lax.Precision.HIGHEST
MESH = pl.DeviceIdType.MESH
VMEM_LIMIT = 56 * 1024 * 1024


def split3(value):
    high = value.astype(BF16)
    rest = value - high.astype(F32)
    middle = rest.astype(BF16)
    low = (rest - middle.astype(F32)).astype(BF16)
    return high, middle, low


def radiances(block, scale_ref, weight_ref, state, column_x_ref, column_y_ref, peak_ref, part, gathered):
    one = slice(block, block + 1)
    column = column_x_ref[one, :] * CY + column_y_ref[one, :]
    first_level = (lax.axis_index("lev") * LEV).astype(F32)
    chosen = (lax.broadcasted_iota(jnp.int32, (COLS, NB), 0) == column).astype(F32)
    chosen = chosen.astype(BF16)
    for level in range(LEV):
        profile = jnp.concatenate(
            [jnp.tanh(state[level * CX + x] * scale_ref[level]) for x in range(CX)], axis=1
        )
        parts = jnp.concatenate(split3(profile), axis=0)
        picked = jnp.dot(parts, chosen, preferred_element_type=F32)
        gathered[level] = picked[:M] + picked[M : 2 * M] + picked[2 * M :]
    peak = peak_ref[one, :].astype(F32)
    shapes = [
        jnp.exp(-jnp.square((first_level + level - peak) / PEAKW)) for level in range(LEV)
    ]

    def produce(channel):
        factors = [shapes[level] * weight_ref[channel, level] for level in range(LEV)]
        for tile in range(4):
            lanes = slice(tile * 128, tile * 128 + 128)
            half, quarter = tile // 2, tile % 2
            total = gathered[0, :, lanes] * factors[0][:, lanes]
            for level in range(1, LEV):
                total += gathered[level, :, lanes] * factors[level][:, lanes]
            part[half, channel, quarter * M : quarter * M + M, :] = total

    return produce


def row_of(kind, level, which):
    return level * CX + which * (3 - 2 * kind) + kind


def place():
    lev, gx, gy = lax.axis_index("lev"), lax.axis_index("gx"), lax.axis_index("gy")
    core, y = lax.rem(lev, 2), lax.div(lev, 2)
    x, z = lax.rem(gy, 4), gx * 2 + lax.div(gy, 4)

    def at(dx, dy, dz, dcore):
        there_x, there_y = lax.rem(x + dx, 4), lax.rem(y + dy, 4)
        there_z, there_core = lax.rem(z + dz, 8), lax.rem(core + dcore, 2)
        return (
            there_y * 2 + there_core,
            lax.div(there_z, 2),
            lax.rem(there_z, 2) * 4 + there_x,
        )

    beside = (
        (lev, lax.rem(gx + 1, 4), gy),
        (lev, lax.rem(gx + 3, 4), gy),
        (lev, gx, lax.rem(gy + 1, 8)),
        (lev, gx, lax.rem(gy + 7, 8)),
    )
    return x, y, z, core, at, beside


def share(block, enter, produce, meanwhile, digest, owner_ref, part, whole, from_core, sums, from_y, from_z, from_x, send, recv):
    x, y, z, core, at, _ = place()
    owner = owner_ref[block]
    owner_z = lax.div(owner, 8) * 2 + lax.div(lax.rem(owner, 8), 4)
    owner_x = lax.rem(owner, 4)
    y_at = lambda d: lax.rem(y + d, 4)
    z_at = lambda d: lax.rem(z + d, 8)
    to_core = at(0, 0, 0, 1)
    to_x = lambda d: at(d, 0, 0, 0)
    to_y = lambda d: at(0, d, 0, 0)
    to_z = lambda d: at(0, 0, d, 0)
    slot = [0]
    started = []

    def start(src, dst, device):
        number = slot[0]
        slot[0] += 1
        copy = pltpu.make_async_remote_copy(
            src_ref=src,
            dst_ref=dst,
            send_sem=send.at[block, number],
            recv_sem=recv.at[block, number],
            device_id=device,
            device_id_type=MESH,
        )
        copy.start()
        started.append(copy)
        return copy

    def arrive(copies):
        for copy in copies:
            copy.wait_recv()

    sent = []

    def pass_on(d, copy):
        copy.wait_recv()
        here = y_at(d)
        sums[here] = part[core, here] + from_core[here]
        if d > 0:
            sent.append(start(sums.at[here], from_y.at[d - 1], to_y(d)))

    before = None
    order = (2, 1, 3, 0)
    if enter is not None:
        for d in order:
            produce(y_at(d))
        meanwhile()
        enter()
    for d in order:
        if enter is None:
            produce(y_at(d))
        copy = start(part.at[1 - core, y_at(d)], from_core.at[y_at(d)], to_core)
        if before is not None:
            pass_on(*before)
        before = d, copy
    pass_on(*before)
    arrive(sent)
    sums[y] = sums[y] + from_y[0] + from_y[1] + from_y[2]

    far_first = (4, 3, 5, 2, 6, 1, 7)
    sent = [
        start(sums.at[y, pl.ds(z_at(d) * PIECE, PIECE)], from_z.at[z], to_z(d))
        for d in far_first
    ]
    mine = pl.ds(pl.multiple_of(z * PIECE, 8), PIECE)
    from_z[z] = sums[y, mine]
    if enter is None:
        meanwhile()
    arrive(sent)
    from_x[x] = from_z[owner_z]
    own = from_x.at[x]
    arrive([start(own, own, to_x(d)) for d in (2, 1, 3)])
    whole[core, y, mine] = from_x[owner_x]
    own = whole.at[core, y, mine]
    arrive([start(own, own, to_z(d)) for d in far_first])
    own = whole.at[core, y]
    sent = {d: start(own, own, to_y(d)) for d in (2, 1, 3)}
    before = start(own, own, to_core), y
    for d in (1, 3, 2):
        sent[d].wait_recv()
        came = whole.at[core, y_at(4 - d)]
        after = start(came, came, to_core), y_at(4 - d)
        before[0].wait_recv()
        digest(before[1])
        before = after
    before[0].wait_recv()
    digest(before[1])
    return started


N_COPIES = 4 + 3 + 7 + 3 + 7 + 3 + 4


def assimilate(
    block,
    owner_ref,
    error_ref,
    state,
    whole,
    observed_ref,
    column_x_ref,
    column_y_ref,
    peak_ref,
    spread,
    scaled,
    innovation,
    pert,
    solved_t,
    taper_y,
    taper_vx,
    system,
    weight,
    share_now,
    then,
):
    owner = owner_ref[block]
    one = slice(block, block + 1)
    cross = []

    def inverse_of(channel):
        return 1.0 / jnp.full((1, 128), error_ref[channel], F32)

    def digest(channel):
        inverse = inverse_of(channel)
        this = lax.broadcasted_iota(jnp.int32, (NCH, 128), 0) == channel
        for tile in range(4):
            half, quarter = tile // 2, tile % 2
            evolved = whole[half, channel, quarter * M : quarter * M + M, :]
            mean = jnp.sum(evolved, axis=0, keepdims=True) * (1.0 / M)
            lanes = slice(tile * 128, tile * 128 + 128)
            part = evolved - mean
            spread[channel, :, lanes] = part
            pert[channel, :, lanes] = part.astype(BF16)
            scaled[:M, lanes] = part * inverse
            wanted = jnp.where(this, observed_ref[block, :, lanes], 0.0)
            away = jnp.sum(wanted, axis=0, keepdims=True) - mean
            innovation[channel, :, lanes] = away
            scaled[M:, lanes] = jnp.broadcast_to(away * inverse, (8, 128))
        cross.append(
            lax.dot_general(
                scaled[...], spread[channel], (((1,), (1,)), ((), ())), precision=HIGHEST,
                preferred_element_type=F32,
            )
        )

    def tapers():
        peak = peak_ref[one, :].astype(F32)
        at_x = lax.div(owner, 8) * CX + column_x_ref[one, :]
        at_y = lax.rem(owner, 8) * CY + column_y_ref[one, :]
        grid_y = lax.axis_index("gy") * CY + lax.broadcasted_iota(jnp.int32, (CY, NB), 0)
        gap = jnp.abs(grid_y - at_y)
        gap = jnp.minimum(gap, 8 * CY - gap).astype(F32)
        taper_y[...] = jnp.exp(-jnp.square(gap / HLOC_Y))
        index = lax.broadcasted_iota(jnp.int32, (ROWS, NB), 0)
        grid_x = lax.axis_index("gx") * CX + lax.rem(index, CX)
        gap = jnp.abs(grid_x - at_x)
        gap = jnp.minimum(gap, 4 * CX - gap).astype(F32)
        level = (lax.axis_index("lev") * LEV + lax.div(index, CX)).astype(F32)
        taper_vx[...] = (
            jnp.exp(-jnp.square((level - peak) / VLOC)) * jnp.exp(-jnp.square(gap / HLOC_X))
        ) * (1.0 / (M - 1))

    started = share_now(tapers, digest)
    cross = cross[0] + cross[1] + cross[2] + cross[3]
    lane = lax.broadcasted_iota(jnp.int32, (M + 8, 128), 1)
    row = lax.broadcasted_iota(jnp.int32, (M + 8, 128), 0)
    cross = jnp.concatenate([cross, jnp.zeros((M + 8, 128 - M), F32)], axis=1)
    system[...] = cross + jnp.where((lane == row) & (row < M), float(M - 1), 0.0)

    def sweep(pair):
        p, q = pair * 2, pair * 2 + 1
        matrix = system[...]
        row_p, row_q = system[pl.ds(p, 1), :], system[pl.ds(q, 1), :]
        at_p, at_q = jnp.full((M + 8, 128), p, jnp.int32), jnp.full((M + 8, 128), q, jnp.int32)
        column_p = jnp.take_along_axis(matrix, at_p, axis=1)
        column_q = jnp.take_along_axis(matrix, at_q, axis=1)
        rows_p, rows_q = jnp.broadcast_to(row_p, (8, 128)), jnp.broadcast_to(row_q, (8, 128))
        pp = jnp.take_along_axis(rows_p, at_p[:8], axis=1)[:1]
        pq = jnp.take_along_axis(rows_p, at_q[:8], axis=1)[:1]
        qq = jnp.take_along_axis(rows_q, at_q[:8], axis=1)[:1]
        inverse = 1.0 / (pp * qq - pq * pq)
        lane_p, lane_q = lane == p, lane == q
        away = lane_p[:1] | lane_q[:1]
        row_p = jnp.where(away, jnp.where(lane_p[:1], -1.0, 0.0), row_p)
        row_q = jnp.where(away, jnp.where(lane_q[:1], -1.0, 0.0), row_q)
        times_p = (qq * inverse) * row_p - (pq * inverse) * row_q
        times_q = (pp * inverse) * row_q - (pq * inverse) * row_p
        is_p, is_q = row == p, row == q
        swept = is_p | is_q
        column_p = jnp.where(swept, jnp.where(is_p, -1.0, 0.0), column_p)
        column_q = jnp.where(swept, jnp.where(is_q, -1.0, 0.0), column_q)
        matrix = jnp.where(swept | lane_p | lane_q, 0.0, matrix)
        system[...] = matrix - column_p * times_p - column_q * times_q

    @pl.loop(0, ROWS // GROUP)
    def _(group):
        for turn in range(STEPS):
            sweep(group * STEPS + turn)
        anomalies = []
        besides = []
        for at in range(GROUP):
            here = row_of(lax.div(group, 4), lax.rem(group, 4) * (GROUP // 2) + at // 2, at % 2)
            member = state[here]
            anomaly = member - jnp.sum(member, axis=0, keepdims=True) * (1.0 / M)
            anomalies.append(anomaly.T.astype(BF16))
            besides.append(taper_vx[pl.ds(here, 1), :])
        anomaly = jnp.concatenate(anomalies, axis=0)
        for chunk in range(NB // HALF):
            near = slice(chunk * HALF, chunk * HALF + HALF)
            taper = jnp.concatenate([taper_y[:, near] * b[:, near] for b in besides], axis=0)
            for channel in range(NCH):
                lanes = slice(channel * NB + chunk * HALF, channel * NB + chunk * HALF + HALF)
                covariance = jnp.dot(
                    anomaly, pert[channel, :, near], preferred_element_type=F32
                )
                rows = pl.ds(group * (GROUP * CY), GROUP * CY)
                weight[rows, lanes] = (taper * covariance).astype(BF16)

    swept = system[...]
    gain = (swept[M : M + 1] - 0.5 * (M - 1) * swept[:M])[:, :M]
    for channel in range(NCH):
        lanes = slice(channel * NB, channel * NB + NB)
        change = jnp.dot(gain, spread[channel], precision=HIGHEST, preferred_element_type=F32)
        solved = inverse_of(channel)[:, :1] * (innovation[channel] - change)
        solved_t[lanes, :] = solved.T.astype(BF16)

    def finish(group):
        update = jnp.dot(
            weight[pl.ds(group * (LAST * CY), LAST * CY), :],
            solved_t[...],
            preferred_element_type=F32,
        )
        for at in range(LAST):
            here = row_of(group // 2, group % 2 * (LAST // 2) + at // 2, at % 2)
            state[here] = state[here] + update[at * CY : at * CY + CY].T

    for group in range(ROWS // LAST):
        finish(group)
        if then is not None:
            then(group)
    for copy in started:
        copy.wait_send()


def transport(speed_x_ref, speed_y_ref, state, out_ref, middle, face, got, edge, came, send, recv):
    targets = place()[-1]
    lane = lax.broadcasted_iota(jnp.int32, (M, CY), 1)
    copies = {}

    def start(key, src, dst, target):
        number = len(copies)
        copies[key] = pltpu.make_async_remote_copy(
            src_ref=src,
            dst_ref=dst,
            send_sem=send.at[number],
            recv_sem=recv.at[number],
            device_id=target,
            device_id_type=MESH,
        )
        copies[key].start()

    def send_faces(turn, half):
        source = middle if turn else state
        for level in range(half * SOME, half * SOME + SOME):
            face[turn, 0, level] = source[level * CX + CX - 1].astype(BF16)
            face[turn, 1, level] = source[level * CX].astype(BF16)
        some = pl.ds(half * SOME, SOME)
        for n in range(2):
            start(("x", turn, half, n), face.at[turn, n, some], got.at[turn, n, some], targets[n])

    def send_edges(turn, kind):
        source = middle if turn else state

        def pack(level, packed):
            for which in range(2):
                slot = level * 2 + which
                turned = pltpu.roll(source[row_of(kind, level, which)], slot * 2 + 2, 1)
                here = (lane == slot * 2 + 1) | (lane == slot * 2 + 2)
                packed = jnp.where(here, turned, packed)
            return packed

        edge[turn, kind] = lax.fori_loop(0, LEV, pack, jnp.zeros((M, CY), F32)).astype(BF16)
        for n in range(2):
            start(
                ("y", turn, kind, n), edge.at[turn, kind], came.at[turn, kind, n], targets[2 + n]
            )

    def take_edges(turn, kind):
        for n in range(2):
            copies["y", turn, kind, n].wait_recv()
        return jnp.where(
            lax.rem(lane, 2) == 1,
            came[turn, kind, 0].astype(F32),
            pltpu.roll(came[turn, kind, 1].astype(F32), CY - 2, 1),
        )

    def advance(turn, kind, edges, level):
        source = middle if turn else state
        for which in range(2):
            at = row_of(kind, level, which)
            centre = source[at]
            u = speed_x_ref[pl.ds(at, 1), :]
            v = speed_y_ref[pl.ds(at, 1), :]
            value = centre * (1.0 - 4.0 * KAPPA - jnp.abs(u) - jnp.abs(v))
            if kind == 1 or which == 1:
                value += source[at - 1] * (jnp.maximum(u, 0.0) + KAPPA)
            if kind == 1 or which == 0:
                value += source[at + 1] * (KAPPA - jnp.minimum(u, 0.0))
            beyond = pltpu.roll(edges, CY - 1 - 2 * (level * 2 + which), 1)
            south = jnp.where(lane == 0, beyond, pltpu.roll(centre, 1, 1))
            north = jnp.where(lane == CY - 1, beyond, pltpu.roll(centre, CY - 1, 1))
            value += south * (jnp.maximum(v, 0.0) + KAPPA) + north * (KAPPA - jnp.minimum(v, 0.0))
            if turn == 0:
                middle[at] = value
            elif kind == 0:
                state[at] = value
            else:
                out_ref[pl.ds(at, M, stride=ROWS), :] = value

    def complete(turn, level):
        for which in range(2):
            at = row_of(0, level, which)
            u = speed_x_ref[pl.ds(at, 1), :]
            factor = KAPPA - jnp.minimum(u, 0.0) if which else jnp.maximum(u, 0.0) + KAPPA
            term = got[turn, which, level].astype(F32) * factor
            if turn == 0:
                middle[at] = middle[at] + term
            else:
                out_ref[pl.ds(at, M, stride=ROWS), :] = state[at] + term

    def alone(turn, kind):
        edges = take_edges(turn, kind)
        pl.loop(0, LEV)(lambda level: advance(turn, kind, edges, level))

    def outer(turn):
        for half in range(LEV // SOME):
            for n in range(2):
                copies["x", turn, half, n].wait_recv()
            pl.loop(half * SOME, half * SOME + SOME)(lambda level: complete(turn, level))
            if turn == 0:
                send_faces(1, half)

    def early(group):
        if group < 2:
            send_faces(0, group)
        if group == 1:
            send_edges(0, 0)
        if group == 3:
            send_edges(0, 1)

    def rest():
        alone(0, 0)
        outer(0)
        send_edges(1, 0)
        alone(0, 1)
        send_edges(1, 1)
        alone(1, 0)
        alone(1, 1)
        outer(1)
        for copy in copies.values():
            copy.wait_send()

    return early, rest


def filter_kernel(
    scale_ref,
    weight_ref,
    error_ref,
    owner_ref,
    ensemble_ref,
    observed_ref,
    column_x_ref,
    column_y_ref,
    peak_ref,
    speed_x_ref,
    speed_y_ref,
    out_ref,
    state,
    gathered,
    part,
    whole_0,
    whole_1,
    from_core_0,
    from_core_1,
    sums,
    from_y_0,
    from_y_1,
    from_z_0,
    from_z_1,
    from_x_0,
    from_x_1,
    spread,
    scaled,
    innovation,
    pert,
    solved_t,
    taper_y,
    taper_vx,
    system,
    weight,
    middle,
    face,
    got,
    edge,
    came,
    send,
    recv,
    face_send,
    face_recv,
    landed,
    load_sem,
):
    load = pltpu.make_async_copy(ensemble_ref, landed, load_sem)
    load.start()
    at, beside = place()[-2:]
    peers = [at(0, 0, 0, 1)] + [at(0, d, 0, 0) for d in range(1, 4)]
    peers += [at(0, 0, d, 0) for d in range(1, 8)] + [at(d, 0, 0, 0) for d in range(1, 4)]
    peers += beside
    barrier = pltpu.get_barrier_semaphore()
    for peer in peers:
        pl.semaphore_signal(barrier, inc=1, device_id=peer, device_id_type=MESH)

    load.wait()
    for row in range(ROWS):
        state[row] = landed[pl.ds(row, M, stride=ROWS), :]

    def enter():
        pl.semaphore_wait(barrier, len(peers))

    early, rest = transport(
        speed_x_ref, speed_y_ref, state, out_ref, middle, face, got, edge, came, face_send,
        face_recv,
    )
    for block in range(NBLK):
        produce = radiances(
            block, scale_ref, weight_ref, state, column_x_ref, column_y_ref, peak_ref, part,
            gathered,
        )
        whole = (whole_0, whole_1)[block]
        from_core = (from_core_0, from_core_1)[block]
        from_y = (from_y_0, from_y_1)[block]
        from_z = (from_z_0, from_z_1)[block]
        from_x = (from_x_0, from_x_1)[block]

        def share_now(meanwhile, digest):
            return share(
                block, enter if block == 0 else None, produce, meanwhile, digest, owner_ref, part, whole, from_core, sums, from_y,
                from_z, from_x, send, recv,
            )

        then = None if block < NBLK - 1 else early
        assimilate(
            block, owner_ref, error_ref, state, whole, observed_ref, column_x_ref, column_y_ref,
            peak_ref, spread, scaled, innovation, pert, solved_t, taper_y, taper_vx, system, weight,
            share_now, then,
        )
    rest()


SMEM_SPEC = pl.BlockSpec(memory_space=pltpu.SMEM)
VMEM_SPEC = pl.BlockSpec(memory_space=pltpu.VMEM)


def shards(
    ensemble,
    level_scale,
    channel_weights,
    error_var,
    observed,
    column_x,
    column_y,
    peak_level,
    owner_map,
    courant_x,
    courant_y,
):
    result = pl.pallas_call(
        filter_kernel,
        out_shape=jax.ShapeDtypeStruct((M * ROWS, CY), F32),
        in_specs=[SMEM_SPEC] * 4 + [pl.BlockSpec(memory_space=pl.ANY)] + [VMEM_SPEC] * 6,
        out_specs=VMEM_SPEC,
        scratch_shapes=[
            pltpu.VMEM((ROWS, M, CY), F32),
            pltpu.VMEM((LEV, M, NB), F32),
            pltpu.VMEM((2, NCH, 2 * M, 128), F32),
            *[pltpu.VMEM((2, NCH, 2 * M, 128), F32)] * NBLK,
            *[pltpu.VMEM((4, 2 * M, 128), F32)] * NBLK,
            pltpu.VMEM((4, 2 * M, 128), F32),
            *[pltpu.VMEM((3, 2 * M, 128), F32)] * NBLK,
            *[pltpu.VMEM((8, PIECE, 128), F32)] * NBLK,
            *[pltpu.VMEM((4, PIECE, 128), F32)] * NBLK,
            pltpu.VMEM((NCH, M, NB), F32),
            pltpu.VMEM((M + 8, NB), F32),
            pltpu.VMEM((NCH, 1, NB), F32),
            pltpu.VMEM((NCH, M, NB), BF16),
            pltpu.VMEM((NCH * NB, M), BF16),
            pltpu.VMEM((CY, NB), F32),
            pltpu.VMEM((ROWS, NB), F32),
            pltpu.VMEM((M + 8, 128), F32),
            pltpu.VMEM((ROWS * CY, NCH * NB), BF16),
            pltpu.VMEM((ROWS, M, CY), F32),
            pltpu.VMEM((2, 2, LEV, M, CY), BF16),
            pltpu.VMEM((2, 2, LEV, M, CY), BF16),
            pltpu.VMEM((2, 2, M, CY), BF16),
            pltpu.VMEM((2, 2, 2, M, CY), BF16),
            pltpu.SemaphoreType.DMA((NBLK, N_COPIES)),
            pltpu.SemaphoreType.DMA((NBLK, N_COPIES)),
            pltpu.SemaphoreType.DMA((N_FACES,)),
            pltpu.SemaphoreType.DMA((N_FACES,)),
            pltpu.VMEM((M * ROWS, CY), F32),
            pltpu.SemaphoreType.DMA,
        ],
        compiler_params=pltpu.CompilerParams(
            vmem_limit_bytes=VMEM_LIMIT, collective_id=0, has_side_effects=True
        ),
        name="filter",
    )(
        level_scale,
        channel_weights,
        error_var,
        owner_map,
        ensemble.reshape(M * ROWS, CY),
        observed,
        column_x,
        column_y,
        peak_level,
        courant_x.reshape(ROWS, CY),
        courant_y.reshape(ROWS, CY),
    )
    return result.reshape(ensemble.shape)


def solution(mesh):
    in_specs = (
        P(None, "lev", "gx", "gy"),
        P("lev"),
        P(None, "lev"),
        P(),
        P(),
        P(),
        P(),
        P(),
        P(),
        P("lev", "gx", "gy"),
        P("lev", "gx", "gy"),
    )
    out_specs = P(None, "lev", "gx", "gy")
    return jax.shard_map(shards, mesh=mesh, in_specs=in_specs, out_specs=out_specs, check_vma=False)
```
